512 devices in a mesh: pool: 2 (over core), seq: 64 (over y, z), tp: 4 (over x).
Axes of the slice: x: 4, y: 4, z: 16, core: 2. Of those that a mesh axis runs over, the one named last changes fastest.
Arguments:
- tokens: bfloat16 [2048, 2560], P('seq'), may hold values from -6 to 6
- query_proj: bfloat16 [2048, 2048], P('seq', ('pool', 'tp')), may hold values from -36 to 36
- key_proj: bfloat16 [2048, 2048], P('seq', ('pool', 'tp')), may hold values from -6 to 6
- value_proj: bfloat16 [2048, 2048], P('seq', ('pool', 'tp')), may hold values from -12 to 12
- w_out: bfloat16 [2048, 2560], P(('pool', 'tp')), may hold values from -0.125 to 0.125
- modulation: float32 [4, 2560], replicated, may hold values from -3 to 3
- expert_ids: int32 [2048, 2], P('seq'), may hold values from 0 to 7, all different within a row; in each aligned block of 32 rows (0 to 31, 32 to 63, ...) at most 14 rows name the same one
- gate_values: float32 [2048, 2], P('seq'), may hold values from 0.1 to 0.9
- w_gate: bfloat16 [8, 2560, 6912], P(('pool', 'tp'), None, 'seq'), may hold values from -0.125 to 0.125
- w_up: bfloat16 [8, 2560, 6912], P(('pool', 'tp'), None, 'seq'), may hold values from -0.125 to 0.125
- w_down: bfloat16 [8, 6912, 2560], P(('pool', 'tp'), 'seq'), may hold values from -0.078125 to 0.078125
Outputs:
- block_out: bfloat16 [2048, 2560], P('seq', ('pool', 'tp'))
The draws below stay inside these ranges and needn't reach their ends.
Inputs may be any that keep to these rules, and one draw needn't show every extreme that they name: `expert_ids`: among the 32 rows of one seq shard, each expert is named by at most 14 rows.
All inputs are finite; a program needn't handle non-finite values.
Results may differ from the reference program's by a relative error of at most 0.02.
Values may be sent and summed in bfloat16 or wider, within the bound.
No kernel may reach another device: no remote copies, remote signals or barrier semaphores. Data moves between devices by JAX's collectives and lax.ppermute only.
A program may use at most 128 MiB of HBM per device.

```python
import math
import jax
import jax.numpy as jnp
import numpy as np
from jax import lax

D = 2560
HEADS = 16
HD = 128
EXPERTS = 8
FF = 6912
TOP = 2
TOK_DEV = 32
TOKENS = 2048
CAP = 14
N_SEQ = 64


def attention_pair(key):
    query_key = jax.random.fold_in(key, 101)
    keys_key = jax.random.fold_in(key, 202)
    array_shape = (TOKENS, HEADS * HD)
    query_out = jnp.clip(1.4 * jax.random.normal(query_key, array_shape, jnp.float32), -6.0, 6.0)
    keys_out = jnp.clip(1.4 * jax.random.normal(keys_key, array_shape, jnp.float32), -6.0, 6.0)
    positions = jnp.arange(TOKENS, dtype=jnp.int32)
    opposite = (positions + TOKENS // 2) % TOKENS
    lift = jnp.where(positions % 4 == 0, 1.5, 0.0).astype(jnp.float32)
    query_out = query_out + lift[:, None] * keys_out[opposite]
    return (query_out, keys_out)


def draw_query_proj(key, part):
    return attention_pair(key)[0].astype(jnp.bfloat16)


def draw_key_proj(key, part):
    return attention_pair(key)[1].astype(jnp.bfloat16)


def levels(own_key, dims, split, low, high):
    level = 1.0
    for axis_at, shards_of in split:
        heights = jax.random.uniform(jax.random.fold_in(jax.random.fold_in(own_key, 6), axis_at), (shards_of,), jnp.float32, low / len(split), high / len(split))
        level = level * jnp.repeat(jnp.exp(heights), dims[axis_at] // shards_of).reshape((-1,) + (1,) * (len(dims) - 1 - axis_at))
    return level


def routed_block(stream_key, own, number, rows, number_of, top, bound, skew):
    sequence = jax.random.permutation(stream_key, number_of)
    crowded, common = portions_of(number_of, rows * top, bound, skew, True), portions_of(number_of, rows * top, bound, skew, False)
    places = jnp.arange(number_of)

    def named(lengths, rotation):
        used = int((lengths > 0).sum())
        fixed = max(1, used // 4)
        shifted = fixed + (places - fixed + rotation * (used - fixed)) % max(1, number_of - fixed)
        return jnp.zeros((number_of,), jnp.int32).at[sequence[jnp.where(places < fixed, places, shifted)]].set(jnp.asarray(lengths, jnp.int32))

    lengths = jnp.where(number % 4 == 0, named(crowded, number // 4), named(common, number - number // 4 - 1))
    mixed = jax.random.permutation(jax.random.fold_in(own, 3), number_of)
    source_of, taker = mixed[0:number_of // 2 * 2:2], mixed[1:number_of // 2 * 2:2]
    slack = jnp.minimum(lengths[source_of] - 1, bound - lengths[taker]) // 2
    slack = jnp.where((source_of == sequence[0]) | (taker == sequence[0]) | (lengths[taker] == 0), 0, jnp.maximum(slack, 0))
    shifted = jax.random.randint(jax.random.fold_in(own, 4), (number_of // 2,), 0, 1 << 20) % (slack + 1)
    lengths = lengths.at[source_of].add(-shifted).at[taker].add(shifted)
    items = jnp.searchsorted(jnp.cumsum(lengths), jnp.arange(rows * top), side="right").astype(jnp.int32)
    listing = items.reshape(top, rows).T
    listing = listing[jax.random.permutation(jax.random.fold_in(own, 1), rows)]
    rotation = jax.random.randint(jax.random.fold_in(own, 2), (rows, 1), 0, top)
    return jnp.take_along_axis(listing, (jnp.arange(top)[None, :] + rotation) % top, axis=1)


def portions_of(count, total, most, skew, full):
    portions = [(1 << 20) // math.isqrt(standing ** skew) + 1 for standing in range(1, count + 1)]
    largest = most if full else min(most, max(-(-total // count), total * portions[0] // sum(portions)))
    least = 1 if total - largest >= count - 1 else 0
    holding, surplus = [largest] + [least] * (count - 1), total - largest - least * (count - 1)
    while surplus > 0:
        free = [i for i in range(1, count) if holding[i] < largest] or [i for i in range(1, count) if holding[i] < most]
        pool, left = sum([portions[i] for i in free]), surplus
        for i in free:
            more = min(most - holding[i], max(1, left * portions[i] // pool), surplus)
            holding[i] = holding[i] + more
            surplus = surplus - more
    return np.array(holding)


def normal_values(stream_key, extent, deviation, limit, cuts=(), kind=jnp.bfloat16):
    values = jax.random.normal(stream_key, extent, jnp.float32) * deviation
    if len(cuts) > 0:
        values = levels(stream_key, extent, cuts, -0.22, 0.18) * values
    return jnp.clip(values, min=-limit, max=limit).astype(kind)


def setup_inputs(seed: int = 0) -> dict:
    seeds = jax.random.split(jax.random.key(seed), 12)
    tokens = normal_values(seeds[0], (TOKENS, D), 1.0, 6.0, ((0, 64),))
    query_proj = draw_query_proj(jax.random.fold_in(seeds[11], 71), 0)
    key_proj = draw_key_proj(jax.random.fold_in(seeds[11], 71), 0)
    value_proj = normal_values(seeds[3], (TOKENS, HEADS * HD), 2.0, 12.0, ((0, 64), (1, 8)))
    w_out = normal_values(seeds[4], (HEADS * HD, D), (HEADS * HD) ** -0.5, 0.125, ((0, 8),))
    modulation = normal_values(seeds[5], (4, D), 0.8, 3.0, (), jnp.float32)
    expert_ids_keys = jax.random.split(jax.random.fold_in(seeds[6], 1), TOKENS // TOK_DEV)
    expert_ids_turns = jax.random.permutation(jax.random.fold_in(seeds[6], 3), TOKENS // TOK_DEV)
    expert_ids = jax.vmap(lambda own, number: routed_block(jax.random.fold_in(seeds[6], 2), own, number, TOK_DEV, EXPERTS, TOP, CAP, 2))(expert_ids_keys, expert_ids_turns).reshape((TOKENS, TOP))
    gate_values = jnp.clip(0.1 + 0.79999997 * jax.random.uniform(seeds[7], (TOKENS, TOP), jnp.float32) ** levels(seeds[7], (TOKENS, TOP), ((0, 64),), -0.2, 0.2), 0.1, 0.9)
    w_gate = normal_values(seeds[8], (EXPERTS, D, FF), D ** -0.5, 0.125, ((0, 8), (2, 64)))
    w_up = normal_values(seeds[9], (EXPERTS, D, FF), D ** -0.5, 0.125, ((0, 8), (2, 64)))
    w_down = normal_values(seeds[10], (EXPERTS, FF, D), FF ** -0.5, 0.078125, ((0, 8), (1, 64)))
    return dict(tokens=tokens, query_proj=query_proj, key_proj=key_proj, value_proj=value_proj, w_out=w_out, modulation=modulation, expert_ids=expert_ids, gate_values=gate_values, w_gate=w_gate, w_up=w_up, w_down=w_down)


def one_head(operands):
    head_query, head_keys, head_values = operands
    scores = jnp.dot(head_query, head_keys.T, preferred_element_type=jnp.float32) * (1.0 / math.sqrt(HD))
    top_score = lax.optimization_barrier(jnp.max(scores, axis=1, keepdims=True))
    exp_scores = jnp.exp(scores - top_score)
    totals = lax.optimization_barrier(jnp.sum(exp_scores, axis=1, keepdims=True))
    weighted = jnp.dot(exp_scores.astype(jnp.bfloat16), head_values, preferred_element_type=jnp.float32)
    return (weighted / totals).astype(jnp.bfloat16)

def one_expert(operands):
    rows_in, gate_mat, up_mat, down_mat = operands
    gated = jnp.dot(rows_in, gate_mat, preferred_element_type=jnp.float32)
    upward = jnp.dot(rows_in, up_mat, preferred_element_type=jnp.float32)
    hidden = (jax.nn.silu(gated) * upward).astype(jnp.bfloat16)
    return jnp.dot(hidden, down_mat, preferred_element_type=jnp.float32)

def reference(tokens, query_proj, key_proj, value_proj, w_out, modulation, expert_ids, gate_values, w_gate, w_up, w_down):
    split_query = query_proj.reshape(TOKENS, HEADS, HD).transpose(1, 0, 2)
    split_keys = key_proj.reshape(TOKENS, HEADS, HD).transpose(1, 0, 2)
    split_values = value_proj.reshape(TOKENS, HEADS, HD).transpose(1, 0, 2)
    heads_out = lax.map(one_head, (split_query, split_keys, split_values))
    heads_out = heads_out.transpose(1, 0, 2).reshape(TOKENS, HEADS * HD)
    attention = jnp.dot(heads_out, w_out, preferred_element_type=jnp.float32)
    resid = tokens.astype(jnp.float32) + modulation[0] * attention
    row_mean = lax.optimization_barrier(jnp.mean(resid, axis=1, keepdims=True))
    row_square = lax.optimization_barrier(jnp.mean(resid * resid, axis=1, keepdims=True))
    inv_dev = lax.rsqrt(row_square - row_mean * row_mean + 1e-06)
    normed = ((resid - row_mean) * inv_dev * (1.0 + modulation[2]) + modulation[1]).astype(jnp.bfloat16)
    expert_range = jnp.arange(EXPERTS, dtype=jnp.int32)
    ids_block = expert_ids.reshape(N_SEQ, TOK_DEV * TOP)
    onehot = (ids_block[:, :, None] == expert_range[None, None, :]).astype(jnp.int32)
    earlier = jnp.cumsum(onehot, axis=1) - onehot
    slot_index = lax.optimization_barrier(jnp.sum(earlier * onehot, axis=2)).reshape(N_SEQ, TOK_DEV, TOP)
    named = expert_ids.reshape(N_SEQ, TOK_DEV, TOP)[:, :, :, None] == expert_range[None, None, None, :]
    placed = slot_index[:, :, :, None] == jnp.arange(CAP, dtype=jnp.int32)[None, None, None, :]
    picked = (named[:, :, :, :, None] & placed[:, :, :, None, :]).astype(jnp.float32)
    dispatch = lax.optimization_barrier(jnp.sum(picked, axis=2))
    combine = lax.optimization_barrier(jnp.sum(gate_values.reshape(N_SEQ, TOK_DEV, TOP)[:, :, :, None, None] * picked, axis=2))
    normed_blocks = normed.reshape(N_SEQ, TOK_DEV, D).astype(jnp.float32)
    buffers = jnp.einsum('stec,std->escd', dispatch, normed_blocks, precision=lax.Precision.HIGHEST).astype(jnp.bfloat16)
    outputs = lax.map(one_expert, (buffers.reshape(EXPERTS, N_SEQ * CAP, D), w_gate, w_up, w_down))
    outputs = outputs.reshape(EXPERTS, N_SEQ, CAP, D)
    mixture = jnp.einsum('stec,escd->std', combine, outputs, precision=lax.Precision.HIGHEST).reshape(TOKENS, D)
    return (resid + modulation[3] * mixture).astype(jnp.bfloat16)
```

```python
import math

import jax
import jax.numpy as jnp
from jax import lax
from jax.experimental import pallas as pl
from jax.experimental.pallas import tpu as pltpu
from jax.sharding import Mesh
from jax.sharding import PartitionSpec as P

HD = 128
Y = 4
Z = 16
TP = 4
GROUP = ("pool", "tp")
F32 = jnp.float32
BF16 = jnp.bfloat16


def spread(x, axis, count):
    copies = jnp.broadcast_to(x[None], (count,) + x.shape)
    return lax.all_to_all(copies, axis, split_axis=0, concat_axis=0, tiled=True)


def exchange(x, axis):
    return lax.all_to_all(x, axis, split_axis=0, concat_axis=0, tiled=True)


def ffn_kernel(x_ref, c_ref, g0, u0, d0, g1, u1, d1, o_ref, acc_ref):
    step = pl.program_id(0)
    share = x_ref.shape[2]
    half = share // 2
    width = share * TP

    @pl.when(step == 0)
    def _():
        acc_ref[...] = jnp.zeros_like(acc_ref)

    total = acc_ref[...]
    for e, (g, u, d) in enumerate(((g0, u0, d0), (g1, u1, d1))):
        gate = jnp.zeros((x_ref.shape[1], g.shape[2]), F32)
        up = gate
        for t in range(TP):
            lo = slice(t * half, (t + 1) * half)
            hi = slice(width // 2 + t * half, width // 2 + (t + 1) * half)
            x = x_ref[t]
            gate += jnp.dot(
                x, jnp.concatenate([g[0, lo], g[0, hi]], 0), preferred_element_type=F32
            )
            up += jnp.dot(x, jnp.concatenate([u[0, lo], u[0, hi]], 0), preferred_element_type=F32)
        act = (gate / (1.0 + jnp.exp(-gate)) * up).astype(BF16)
        total += c_ref[:, e : e + 1] * jnp.dot(act, d[0], preferred_element_type=F32)
    acc_ref[...] = total

    @pl.when(step == Y - 1)
    def _():
        for t in range(TP):
            lo = acc_ref[:, t * half : (t + 1) * half]
            hi = acc_ref[:, width // 2 + t * half : width // 2 + (t + 1) * half]
            o_ref[t] = jnp.concatenate([lo, hi], 1).astype(BF16)


def ffn(x, weights, mine, other):
    tp, rows, share = x.shape
    width = tp * share
    hidden = mine[0].shape[2]
    wide = pl.BlockSpec((1, width, hidden), lambda i: (i, 0, 0))
    tall = pl.BlockSpec((1, hidden, width), lambda i: (i, 0, 0))
    return pl.pallas_call(
        ffn_kernel,
        grid=(Y,),
        out_shape=jax.ShapeDtypeStruct((tp, rows, share), BF16),
        in_specs=[
            pl.BlockSpec((tp, rows, share), lambda i: (0, 0, 0)),
            pl.BlockSpec(weights.shape, lambda i: (0, 0)),
            wide,
            wide,
            tall,
            wide,
            wide,
            tall,
        ],
        out_specs=pl.BlockSpec((tp, rows, share), lambda i: (0, 0, 0)),
        scratch_shapes=[pltpu.VMEM((rows, width), F32)],
        compiler_params=pltpu.CompilerParams(vmem_limit_bytes=48 << 20),
        cost_estimate=pl.CostEstimate(
            flops=12 * rows * width * hidden * Y,
            bytes_accessed=12 * width * hidden * Y,
            transcendentals=0,
        ),
    )(x, weights, *mine, *other)


def body(
    tokens,
    query_proj,
    key_proj,
    value_proj,
    w_out,
    modulation,
    expert_ids,
    gate_values,
    w_gate,
    w_up,
    w_down,
):
    rows, width = tokens.shape
    heads = query_proj.shape[1] // HD
    half_rows = rows // 2
    share = width // TP
    pool = lax.axis_index("pool")
    tp = lax.axis_index("tp")

    mine = [lax.all_gather(w[0], "y", axis=0) for w in (w_gate, w_up, w_down)]
    other = [lax.ppermute(w, "pool", [(0, 1), (1, 0)]) for w in mine]

    key_value = lax.all_gather(
        jnp.concatenate([key_proj, value_proj], 1), "z", axis=0, tiled=True
    )
    queries = spread(query_proj, "y", Y).reshape(Y * rows, heads * HD)
    parts = []
    stats = []
    for h in range(heads):
        cols = slice(h * HD, (h + 1) * HD)
        keys = key_value[:, cols]
        values = key_value[:, heads * HD + h * HD : heads * HD + (h + 1) * HD]
        scores = lax.dot_general(
            queries[:, cols], keys, (((1,), (1,)), ((), ())), preferred_element_type=F32
        ) * (1.0 / math.sqrt(HD))
        top = jnp.max(scores, axis=1, keepdims=True)
        weights = jnp.exp(scores - top)
        stats += [top, jnp.sum(weights, axis=1, keepdims=True)]
        parts.append(jnp.dot(weights.astype(BF16), values, preferred_element_type=F32))
    stats = jnp.concatenate(stats, 1)
    stats = jnp.pad(stats, ((0, 0), (0, HD - stats.shape[1])))
    packed = jnp.concatenate(parts + [stats], 1).reshape(Y, rows, (heads + 1) * HD)
    packed = exchange(packed, "y")
    outs = []
    for h in range(heads):
        acc = packed[:, :, h * HD : (h + 1) * HD]
        top = packed[:, :, heads * HD + 2 * h : heads * HD + 2 * h + 1]
        part_total = packed[:, :, heads * HD + 2 * h + 1 : heads * HD + 2 * h + 2]
        scale = jnp.exp(top - jnp.max(top, axis=0, keepdims=True))
        outs.append(jnp.sum(scale * acc, axis=0) / jnp.sum(scale * part_total, axis=0))
    heads_out = jnp.concatenate(outs, 1).astype(BF16)

    projected = jnp.dot(heads_out, w_out, preferred_element_type=F32).astype(BF16)
    projected = projected.reshape(2, half_rows, 2, TP, share // 2).transpose(0, 3, 1, 2, 4)
    projected = exchange(projected.reshape(2 * TP, half_rows, share), GROUP)
    attention = jnp.sum(projected.astype(F32), axis=0).astype(BF16)
    attention = spread(attention, "tp", TP)
    attention = (
        attention.reshape(TP, half_rows, 2, share // 2)
        .transpose(1, 2, 0, 3)
        .reshape(half_rows, width)
        .astype(F32)
    )
    half_tokens = lax.dynamic_slice_in_dim(tokens, pool * half_rows, half_rows, 0).astype(F32)
    resid = half_tokens + modulation[0] * attention
    row_mean = jnp.mean(resid, axis=1, keepdims=True)
    row_square = jnp.mean(resid * resid, axis=1, keepdims=True)
    inv_dev = lax.rsqrt(row_square - row_mean * row_mean + 1e-06)
    normed = ((resid - row_mean) * inv_dev * (1.0 + modulation[2]) + modulation[1]).astype(BF16)

    def my_share(a):
        a = a.reshape(a.shape[0], 2, TP, share // 2)
        return lax.dynamic_index_in_dim(a, tp, 2, keepdims=False).reshape(a.shape[0], share)

    normed_share = my_share(normed)
    resid_share = my_share(resid)
    modul_share = my_share(modulation[3:4])

    half_ids = lax.dynamic_slice_in_dim(expert_ids, pool * half_rows, half_rows, 0)
    half_gates = lax.dynamic_slice_in_dim(gate_values, pool * half_rows, half_rows, 0)
    gates_hi = lax.reduce_precision(half_gates, 8, 7)
    gates_lo = half_gates - gates_hi
    route = jnp.concatenate(
        [half_ids.astype(BF16), gates_hi.astype(BF16), gates_lo.astype(BF16)], 1
    )
    route = jnp.pad(route, ((0, 0), (0, HD - route.shape[1])))
    sent = jnp.concatenate([normed_share, route], 1)
    ring = spread(sent, "z", Z).reshape(Z * half_rows, share + HD)
    rows_in = spread(ring[:, :share], "tp", TP)
    route = ring[:, share : share + 6].astype(F32)
    gates = route[:, 2:4] + route[:, 4:6]
    mine_id = (pool * TP + tp).astype(F32)
    other_id = ((1 - pool) * TP + tp).astype(F32)
    gate_of = [
        jnp.sum(jnp.where(route[:, :2] == e, gates, 0.0), axis=1, keepdims=True)
        for e in (mine_id, other_id)
    ]
    gate_of = jnp.concatenate(gate_of, 1)

    mixed = ffn(rows_in, gate_of, mine, other)
    mixed = jnp.sum(exchange(mixed, "tp").astype(F32), axis=0).astype(BF16)
    mixed = mixed.reshape(Z, half_rows, 2, share // 2).transpose(2, 0, 1, 3)
    mixed = exchange(mixed.reshape(2 * Z, half_rows, share // 2), ("pool", "z"))
    mixture = jnp.sum(mixed.reshape(2, Z, half_rows, share // 2).astype(F32), axis=1)
    mixture = mixture.reshape(rows, share // 2)

    resid_halves = resid_share.reshape(half_rows, 2, share // 2)
    give = lax.dynamic_index_in_dim(resid_halves, 1 - pool, 1, keepdims=False)
    keep = lax.dynamic_index_in_dim(resid_halves, pool, 1, keepdims=False)
    got = lax.ppermute(give, "pool", [(0, 1), (1, 0)])
    resid_out = jnp.where(
        pool == 0, jnp.concatenate([keep, got], 0), jnp.concatenate([got, keep], 0)
    )
    modul_out = lax.dynamic_index_in_dim(
        modul_share.reshape(2, share // 2), pool, 0, keepdims=False
    )
    return (resid_out + modul_out * mixture).astype(BF16)


def solution(mesh):
    split = Mesh(
        mesh.devices.reshape(2, Y, Z, TP), ("pool", "y", "z", "tp")
    )
    seq = ("y", "z")
    in_specs = (
        P(seq, None),
        P(seq, GROUP),
        P(seq, GROUP),
        P(seq, GROUP),
        P(GROUP, None),
        P(),
        P(seq, None),
        P(seq, None),
        P(GROUP, None, seq),
        P(GROUP, None, seq),
        P(GROUP, seq, None),
    )
    return jax.shard_map(
        body, mesh=split, in_specs=in_specs, out_specs=P(seq, GROUP), check_vma=False
    )
```

```python
import math

import jax
import jax.numpy as jnp
from jax import lax
from jax.experimental import pallas as pl
from jax.experimental.pallas import tpu as pltpu
from jax.sharding import Mesh
from jax.sharding import PartitionSpec as P

HD = 128
Y = 4
Z = 16
TP = 4
GROUP = ("pool", "tp")
F32 = jnp.float32
BF16 = jnp.bfloat16


def spread(x, axis, count):
    copies = jnp.broadcast_to(x[None], (count,) + x.shape)
    return lax.all_to_all(copies, axis, split_axis=0, concat_axis=0, tiled=True)


def exchange(x, axis):
    return lax.all_to_all(x, axis, split_axis=0, concat_axis=0, tiled=True)


def pack_weights(w_gate, w_up, w_down):
    pad = -w_down.shape[0] % 16
    return jnp.concatenate(
        [jnp.pad(w, ((0, pad), (0, 0))) for w in (w_gate.T, w_up.T, w_down)], 0
    )


def ffn_kernel(ids_ref, x_ref, mine_ref, other_ref, o_ref, acc_ref):
    step = pl.program_id(0)
    width = o_ref.shape[1]
    hidden = mine_ref.shape[1] // 3

    @pl.when(step == 0)
    def _():
        acc_ref[...] = jnp.zeros_like(acc_ref)

    x = x_ref[:, :width]
    route = x_ref[:, width:].astype(F32)
    total = acc_ref[...]
    for e, w in enumerate((mine_ref, other_ref)):
        both = lax.dot_general(
            x, w[0, : 2 * hidden], (((1,), (1,)), ((), ())), preferred_element_type=F32
        )
        gate = both[:, :hidden]
        act = (gate / (1.0 + jnp.exp(-gate)) * both[:, hidden:]).astype(BF16)
        scale = jnp.zeros((x.shape[0], 1), F32)
        for k in range(2):
            value = route[:, 2 + k : 3 + k] + route[:, 4 + k : 5 + k]
            scale += jnp.where(route[:, k : k + 1] == ids_ref[e].astype(F32), value, 0.0)
        total += scale * jnp.dot(act, w[0, 2 * hidden :], preferred_element_type=F32)
    acc_ref[...] = total

    @pl.when(step == pl.num_programs(0) - 1)
    def _():
        o_ref[...] = total.astype(BF16)


def ffn(ids, x, mine, other):
    rows = x.shape[0]
    steps, depth, width = mine.shape
    weights = pl.BlockSpec((1, depth, width), lambda i: (i, 0, 0))
    return pl.pallas_call(
        ffn_kernel,
        grid=(steps,),
        out_shape=jax.ShapeDtypeStruct((rows, width), BF16),
        in_specs=[
            pl.BlockSpec(memory_space=pltpu.SMEM),
            pl.BlockSpec(x.shape, lambda i: (0, 0)),
            weights,
            weights,
        ],
        out_specs=pl.BlockSpec((rows, width), lambda i: (0, 0)),
        scratch_shapes=[pltpu.VMEM((rows, width), F32)],
        compiler_params=pltpu.CompilerParams(vmem_limit_bytes=58 << 20),
        cost_estimate=pl.CostEstimate(
            flops=4 * rows * width * depth * steps,
            bytes_accessed=4 * width * depth * steps,
            transcendentals=0,
        ),
    )(ids, x, mine, other)


def body(
    tokens,
    query_proj,
    key_proj,
    value_proj,
    w_out,
    modulation,
    expert_ids,
    gate_values,
    w_gate,
    w_up,
    w_down,
):
    rows, width = tokens.shape
    heads = query_proj.shape[1] // HD
    own_rows = rows // (2 * TP)
    pool = lax.axis_index("pool")
    tp = lax.axis_index("tp")
    group = pool * TP + tp

    packed = pack_weights(w_gate[0], w_up[0], w_down[0])
    mine = lax.all_gather(packed, "y", axis=0)

    key_value = spread(jnp.concatenate([key_proj, value_proj], 1), "z", Z)
    key_value = key_value.reshape(Z * rows, 2 * heads * HD)
    queries = spread(query_proj, "y", Y).reshape(Y * rows, heads * HD)
    parts = []
    stats = []
    for h in range(heads):
        cols = slice(h * HD, (h + 1) * HD)
        keys = key_value[:, cols]
        values = key_value[:, heads * HD + h * HD : heads * HD + (h + 1) * HD]
        scores = lax.dot_general(
            queries[:, cols], keys, (((1,), (1,)), ((), ())), preferred_element_type=F32
        ) * (1.0 / math.sqrt(HD))
        top = jnp.max(scores, axis=1, keepdims=True)
        weights = jnp.exp(scores - top)
        stats += [top, jnp.sum(weights, axis=1, keepdims=True)]
        parts.append(jnp.dot(weights.astype(BF16), values, preferred_element_type=F32))
    stats = jnp.concatenate(stats, 1)
    stats = jnp.pad(stats, ((0, 0), (0, HD - stats.shape[1])))
    partial = jnp.concatenate(parts + [stats], 1).reshape(Y, rows, (heads + 1) * HD)
    partial = exchange(partial, "y")
    outs = []
    for h in range(heads):
        acc = partial[:, :, h * HD : (h + 1) * HD]
        top = partial[:, :, heads * HD + 2 * h : heads * HD + 2 * h + 1]
        part_total = partial[:, :, heads * HD + 2 * h + 1 : heads * HD + 2 * h + 2]
        scale = jnp.exp(top - jnp.max(top, axis=0, keepdims=True))
        outs.append(jnp.sum(scale * acc, axis=0) / jnp.sum(scale * part_total, axis=0))
    heads_out = jnp.concatenate(outs, 1).astype(BF16)

    projected = jnp.dot(heads_out, w_out, preferred_element_type=F32).astype(BF16)
    projected = exchange(projected.reshape(2 * TP, own_rows, width), GROUP)
    attention = jnp.sum(projected.astype(F32), axis=0)
    own_tokens = lax.dynamic_slice_in_dim(tokens, group * own_rows, own_rows, 0).astype(F32)
    resid = own_tokens + modulation[0] * attention
    row_mean = jnp.mean(resid, axis=1, keepdims=True)
    row_square = jnp.mean(resid * resid, axis=1, keepdims=True)
    inv_dev = lax.rsqrt(row_square - row_mean * row_mean + 1e-06)
    normed = ((resid - row_mean) * inv_dev * (1.0 + modulation[2]) + modulation[1]).astype(BF16)

    own_ids = lax.dynamic_slice_in_dim(expert_ids, group * own_rows, own_rows, 0)
    own_gates = lax.dynamic_slice_in_dim(gate_values, group * own_rows, own_rows, 0)
    gates_hi = lax.reduce_precision(own_gates, 8, 7)
    gates_lo = own_gates - gates_hi
    route = jnp.concatenate(
        [own_ids.astype(BF16), gates_hi.astype(BF16), gates_lo.astype(BF16)], 1
    )
    route = jnp.pad(route, ((0, 0), (0, HD - route.shape[1])))
    sent = jnp.concatenate([normed, route], 1)
    ring = spread(sent, "z", Z).reshape(Z * own_rows, width + HD)
    mine, ring = lax.optimization_barrier((mine, ring))
    other = lax.ppermute(mine, "pool", [(0, 1), (1, 0)])
    rows_in = spread(ring, "tp", TP).reshape(TP * Z * own_rows, width + HD)
    ids = jnp.stack([group, (1 - pool) * TP + tp]).astype(jnp.int32)
    mixed = ffn(ids, rows_in, mine, other)

    mixed = exchange(mixed.reshape(TP, Z * own_rows, width), "tp")
    mixed = jnp.sum(mixed.astype(F32), axis=0).astype(BF16)
    mixed = exchange(mixed.reshape(Z, own_rows, width), "z")
    mixture = jnp.sum(mixed.astype(F32), axis=0)
    block_out = (resid + modulation[3] * mixture).astype(BF16)
    block_out = block_out.reshape(own_rows, 2 * TP, width // (2 * TP)).transpose(1, 0, 2)
    return exchange(block_out, GROUP).reshape(rows, width // (2 * TP))


def solution(mesh):
    split = Mesh(
        mesh.devices.reshape(2, Y, Z, TP), ("pool", "y", "z", "tp")
    )
    seq = ("y", "z")
    in_specs = (
        P(seq, None),
        P(seq, GROUP),
        P(seq, GROUP),
        P(seq, GROUP),
        P(GROUP, None),
        P(),
        P(seq, None),
        P(seq, None),
        P(GROUP, None, seq),
        P(GROUP, None, seq),
        P(GROUP, seq, None),
    )
    return jax.shard_map(
        body, mesh=split, in_specs=in_specs, out_specs=P(seq, GROUP), check_vma=False
    )
```

```python
import math

import jax
import jax.numpy as jnp
from jax import lax
from jax.experimental import pallas as pl
from jax.experimental.pallas import tpu as pltpu
from jax.sharding import Mesh
from jax.sharding import PartitionSpec as P

HD = 128
Y = 4
ZHI = 4
ZLO = 4
Z = ZHI * ZLO
RING = ("zhi", "zlo")
TP = 4
GROUP = ("pool", "tp")
F32 = jnp.float32
BF16 = jnp.bfloat16


def copies_of(x, count):
    return jnp.broadcast_to(x[None], (count,) + x.shape)


def spread(x, axis, count):
    return exchange(copies_of(x, count), axis)


def exchange(x, axis):
    return lax.all_to_all(x, axis, split_axis=0, concat_axis=0, tiled=True)


def pack_weights(w_gate, w_up, w_down):
    pad = -w_down.shape[0] % 16
    return jnp.concatenate(
        [jnp.pad(w, ((0, pad), (0, 0))) for w in (w_gate.T, w_up.T, w_down)], 0
    )


def ffn_kernel(ids_ref, x_ref, mine_ref, other_ref, o_ref, xt_ref, act_ref, down_ref):
    step = pl.program_id(0)
    width = o_ref.shape[1]
    hidden = mine_ref.shape[1] // 3
    weights = [
        (e, w, s) for s in range(mine_ref.shape[0]) for e, w in enumerate((mine_ref, other_ref))
    ]

    @pl.when(step == 0)
    def _():
        xt_ref[...] = x_ref[...].T

    route = xt_ref[width : width + 16].astype(F32)
    scales = []
    for e in range(2):
        scale = jnp.zeros((1, x_ref.shape[0]), F32)
        for k in range(2):
            value = route[2 + k : 3 + k] + route[4 + k : 5 + k]
            scale += jnp.where(route[k : k + 1] == ids_ref[e].astype(F32), value, 0.0)
        scales.append(scale)
    both = jnp.dot(
        jnp.concatenate([w[s, : 2 * hidden] for _, w, s in weights], 0),
        xt_ref[:width],
        preferred_element_type=F32,
    )
    acts = []
    for i, (e, _, _) in enumerate(weights):
        gate = both[2 * i * hidden : (2 * i + 1) * hidden]
        up = both[(2 * i + 1) * hidden : (2 * i + 2) * hidden]
        acts.append((gate / (1.0 + jnp.exp(-gate)) * up * scales[e]).astype(BF16))
    units = len(weights) * hidden
    here = pl.ds(pl.multiple_of(step * units, 16), units)
    act_ref[here] = jnp.concatenate(acts, 0)
    down_ref[here] = jnp.concatenate([w[s, 2 * hidden :] for _, w, s in weights], 0)

    @pl.when(step == pl.num_programs(0) - 1)
    def _():
        o_ref[...] = lax.dot_general(
            act_ref[...], down_ref[...], (((0,), (0,)), ((), ())), preferred_element_type=F32
        ).astype(BF16)


def ffn(ids, x, mine, other):
    rows = x.shape[0]
    parts, depth, width = mine.shape
    each = 2
    units = 2 * parts * (depth // 3)
    weights = pl.BlockSpec((each, depth, width), lambda i: (i, 0, 0))
    return pl.pallas_call(
        ffn_kernel,
        grid=(parts // each,),
        out_shape=jax.ShapeDtypeStruct((rows, width), BF16),
        in_specs=[
            pl.BlockSpec(memory_space=pltpu.SMEM),
            pl.BlockSpec(x.shape, lambda i: (0, 0)),
            weights,
            weights,
        ],
        out_specs=pl.BlockSpec((rows, width), lambda i: (0, 0)),
        scratch_shapes=[
            pltpu.VMEM((x.shape[1], rows), BF16),
            pltpu.VMEM((units, rows), BF16),
            pltpu.VMEM((units, width), BF16),
        ],
        compiler_params=pltpu.CompilerParams(vmem_limit_bytes=58 << 20),
        cost_estimate=pl.CostEstimate(
            flops=4 * rows * width * depth * parts,
            bytes_accessed=4 * width * depth * parts,
            transcendentals=0,
        ),
    )(ids, x, mine, other)


def body(
    tokens,
    query_proj,
    key_proj,
    value_proj,
    w_out,
    modulation,
    expert_ids,
    gate_values,
    w_gate,
    w_up,
    w_down,
):
    rows, width = tokens.shape
    heads = query_proj.shape[1] // HD
    own_rows = rows // (2 * TP)
    pool = lax.axis_index("pool")
    tp = lax.axis_index("tp")
    group = pool * TP + tp

    mine = lax.all_gather(pack_weights(w_gate[0], w_up[0], w_down[0]), "y", axis=0)

    blocks = [query_proj] + [
        lax.ppermute(query_proj, "zhi", [(i, (i - k) % ZHI) for i in range(ZHI)])
        for k in range(1, ZHI)
    ]
    first = (ZHI - lax.axis_index("zhi")) % ZHI * rows
    queries = lax.dynamic_slice_in_dim(
        jnp.concatenate(blocks + blocks[: ZHI - 1], 0), first, ZHI * rows, 0
    )
    copies = copies_of(jnp.concatenate([key_proj, value_proj], 1), Y * ZLO)
    key_value = exchange(copies, ("y", "zlo")).reshape(Y * ZLO * rows, 2 * heads * HD)
    parts = []
    stats = []
    for h in range(heads):
        cols = slice(h * HD, (h + 1) * HD)
        keys = key_value[:, cols]
        values = key_value[:, heads * HD + h * HD : heads * HD + (h + 1) * HD]
        scores = lax.dot_general(
            queries[:, cols], keys, (((1,), (1,)), ((), ())), preferred_element_type=F32
        ) * (1.0 / math.sqrt(HD))
        top = jnp.max(scores, axis=1, keepdims=True)
        weights = jnp.exp(scores - top)
        total = jnp.sum(weights, axis=1, keepdims=True)
        part = jnp.dot(weights.astype(BF16), values, preferred_element_type=F32)
        parts.append((part / total).astype(BF16))
        log_sum = top + jnp.log(total)
        high = lax.reduce_precision(log_sum, 8, 7)
        middle = lax.reduce_precision(log_sum - high, 8, 7)
        stats += [high, middle, log_sum - high - middle]
    stats = jnp.concatenate(stats, 1).astype(BF16)
    stats = jnp.pad(stats, ((0, 0), (0, HD - stats.shape[1])))
    partial = jnp.concatenate(parts + [stats], 1).reshape(ZHI, rows, (heads + 1) * HD)
    partial = exchange(partial, "zhi").astype(F32)
    outs = []
    for h in range(heads):
        log_sum = partial[:, :, heads * HD + 3 * h : heads * HD + 3 * h + 3]
        log_sum = jnp.sum(log_sum, axis=2, keepdims=True)
        scale = jnp.exp(log_sum - jnp.max(log_sum, axis=0, keepdims=True))
        acc = jnp.sum(scale * partial[:, :, h * HD : (h + 1) * HD], axis=0)
        outs.append(acc / jnp.sum(scale, axis=0))
    heads_out = jnp.concatenate(outs, 1).astype(BF16)

    projected = jnp.dot(heads_out, w_out, preferred_element_type=F32).astype(BF16)
    projected = exchange(projected.reshape(2 * TP, own_rows, width), GROUP)
    attention = jnp.sum(projected.astype(F32), axis=0)
    own_tokens = lax.dynamic_slice_in_dim(tokens, group * own_rows, own_rows, 0).astype(F32)
    resid = own_tokens + modulation[0] * attention
    row_mean = jnp.mean(resid, axis=1, keepdims=True)
    row_square = jnp.mean(resid * resid, axis=1, keepdims=True)
    inv_dev = lax.rsqrt(row_square - row_mean * row_mean + 1e-06)
    normed = ((resid - row_mean) * inv_dev * (1.0 + modulation[2]) + modulation[1]).astype(BF16)

    own_ids = lax.dynamic_slice_in_dim(expert_ids, group * own_rows, own_rows, 0)
    own_gates = lax.dynamic_slice_in_dim(gate_values, group * own_rows, own_rows, 0)
    gates_hi = lax.reduce_precision(own_gates, 8, 7)
    gates_lo = own_gates - gates_hi
    route = jnp.concatenate(
        [own_ids.astype(BF16), gates_hi.astype(BF16), gates_lo.astype(BF16)], 1
    )
    route = jnp.pad(route, ((0, 0), (0, HD - route.shape[1])))
    sent = jnp.concatenate([normed, route], 1)
    ring = spread(sent, RING, Z).reshape(Z * own_rows, width + HD)
    mine, ring = lax.optimization_barrier((mine, ring))
    other = lax.ppermute(mine, "pool", [(0, 1), (1, 0)])
    rows_in = spread(ring, "tp", TP).reshape(TP * Z * own_rows, width + HD)
    ids = jnp.stack([group, (1 - pool) * TP + tp]).astype(jnp.int32)
    mixed = ffn(ids, rows_in, mine, other)

    mixed = exchange(mixed.reshape(TP, Z * own_rows, width), "tp")
    mixed = jnp.sum(mixed.astype(F32), axis=0).astype(BF16)
    mixed = exchange(mixed.reshape(Z, own_rows, width), RING)
    mixture = jnp.sum(mixed.astype(F32), axis=0)
    block_out = (resid + modulation[3] * mixture).astype(BF16)
    block_out = block_out.reshape(own_rows, 2 * TP, width // (2 * TP)).transpose(1, 0, 2)
    return exchange(block_out, GROUP).reshape(rows, width // (2 * TP))


def solution(mesh):
    split = Mesh(
        mesh.devices.reshape(2, Y, ZHI, ZLO, TP), ("pool", "y", "zhi", "zlo", "tp")
    )
    seq = ("y", "zhi", "zlo")
    in_specs = (
        P(seq, None),
        P(seq, GROUP),
        P(seq, GROUP),
        P(seq, GROUP),
        P(GROUP, None),
        P(),
        P(seq, None),
        P(seq, None),
        P(GROUP, None, seq),
        P(GROUP, None, seq),
        P(GROUP, seq, None),
    )
    return jax.shard_map(
        body, mesh=split, in_specs=in_specs, out_specs=P(seq, GROUP), check_vma=False
    )
```

```python
import math

import jax
import jax.numpy as jnp
from jax import lax
from jax.experimental import pallas as pl
from jax.experimental.pallas import tpu as pltpu
from jax.sharding import Mesh
from jax.sharding import PartitionSpec as P

HD = 128
Y = 4
Z = 16
TP = 4
GROUP = ("pool", "tp")
F32 = jnp.float32
BF16 = jnp.bfloat16


def copies_of(x, count):
    return jnp.broadcast_to(x[None], (count,) + x.shape)


def spread(x, axis, count):
    return exchange(copies_of(x, count), axis)


def exchange(x, axis):
    return lax.all_to_all(x, axis, split_axis=0, concat_axis=0, tiled=True)


def pack_weights(w_gate, w_up, w_down):
    pad = -w_down.shape[0] % 16
    return jnp.concatenate(
        [jnp.pad(w, ((0, pad), (0, 0))) for w in (w_gate.T, w_up.T, w_down)], 0
    )


def ffn_kernel(ids_ref, x_ref, mine_ref, other_ref, o_ref, xt_ref, act_ref, down_ref):
    step = pl.program_id(0)
    width = o_ref.shape[1]
    hidden = mine_ref.shape[1] // 3
    weights = [
        (e, w, s) for s in range(mine_ref.shape[0]) for e, w in enumerate((mine_ref, other_ref))
    ]

    @pl.when(step == 0)
    def _():
        xt_ref[...] = x_ref[...].T

    route = xt_ref[width : width + 16].astype(F32)
    scales = []
    for e in range(2):
        scale = jnp.zeros((1, x_ref.shape[0]), F32)
        for k in range(2):
            value = route[2 + k : 3 + k] + route[4 + k : 5 + k]
            scale += jnp.where(route[k : k + 1] == ids_ref[e].astype(F32), value, 0.0)
        scales.append(scale)
    both = jnp.dot(
        jnp.concatenate([w[s, : 2 * hidden] for _, w, s in weights], 0),
        xt_ref[:width],
        preferred_element_type=F32,
    )
    acts = []
    for i, (e, _, _) in enumerate(weights):
        gate = both[2 * i * hidden : (2 * i + 1) * hidden]
        up = both[(2 * i + 1) * hidden : (2 * i + 2) * hidden]
        acts.append((gate / (1.0 + jnp.exp(-gate)) * up * scales[e]).astype(BF16))
    units = len(weights) * hidden
    here = pl.ds(pl.multiple_of(step * units, 16), units)
    act_ref[here] = jnp.concatenate(acts, 0)
    down_ref[here] = jnp.concatenate([w[s, 2 * hidden :] for _, w, s in weights], 0)

    @pl.when(step == pl.num_programs(0) - 1)
    def _():
        o_ref[...] = lax.dot_general(
            act_ref[...], down_ref[...], (((0,), (0,)), ((), ())), preferred_element_type=F32
        ).astype(BF16)


def ffn(ids, x, mine, other):
    rows = x.shape[0]
    parts, depth, width = mine.shape
    each = 2
    units = 2 * parts * (depth // 3)
    weights = pl.BlockSpec((each, depth, width), lambda i: (i, 0, 0))
    return pl.pallas_call(
        ffn_kernel,
        grid=(parts // each,),
        out_shape=jax.ShapeDtypeStruct((rows, width), BF16),
        in_specs=[
            pl.BlockSpec(memory_space=pltpu.SMEM),
            pl.BlockSpec(x.shape, lambda i: (0, 0)),
            weights,
            weights,
        ],
        out_specs=pl.BlockSpec((rows, width), lambda i: (0, 0)),
        scratch_shapes=[
            pltpu.VMEM((x.shape[1], rows), BF16),
            pltpu.VMEM((units, rows), BF16),
            pltpu.VMEM((units, width), BF16),
        ],
        compiler_params=pltpu.CompilerParams(vmem_limit_bytes=58 << 20),
        cost_estimate=pl.CostEstimate(
            flops=4 * rows * width * depth * parts,
            bytes_accessed=4 * width * depth * parts,
            transcendentals=0,
        ),
    )(ids, x, mine, other)


def body(
    tokens,
    query_proj,
    key_proj,
    value_proj,
    w_out,
    modulation,
    expert_ids,
    gate_values,
    w_gate,
    w_up,
    w_down,
):
    rows, width = tokens.shape
    heads = query_proj.shape[1] // HD
    own_rows = rows // (2 * TP)
    pool = lax.axis_index("pool")
    tp = lax.axis_index("tp")
    group = pool * TP + tp

    mine = lax.all_gather(pack_weights(w_gate[0], w_up[0], w_down[0]), "y", axis=0)

    queries = spread(query_proj, "y", Y).reshape(Y * rows, heads * HD)
    key_value = lax.all_gather(
        jnp.concatenate([key_proj, value_proj], 1), "z", axis=0, tiled=True
    )
    parts = []
    stats = []
    for h in range(heads):
        cols = slice(h * HD, (h + 1) * HD)
        keys = key_value[:, cols]
        values = key_value[:, heads * HD + h * HD : heads * HD + (h + 1) * HD]
        scores = lax.dot_general(
            queries[:, cols], keys, (((1,), (1,)), ((), ())), preferred_element_type=F32
        ) * (1.0 / math.sqrt(HD))
        top = jnp.max(scores, axis=1, keepdims=True)
        weights = jnp.exp(scores - top)
        total = jnp.sum(weights, axis=1, keepdims=True)
        part = jnp.dot(weights.astype(BF16), values, preferred_element_type=F32)
        parts.append((part / total).astype(BF16))
        log_sum = top + jnp.log(total)
        high = lax.reduce_precision(log_sum, 8, 7)
        middle = lax.reduce_precision(log_sum - high, 8, 7)
        stats += [high, middle, log_sum - high - middle]
    stats = jnp.concatenate(stats, 1).astype(BF16)
    stats = jnp.pad(stats, ((0, 0), (0, HD - stats.shape[1])))
    partial = jnp.concatenate(parts + [stats], 1).reshape(Y, rows, (heads + 1) * HD)
    partial = exchange(partial, "y").astype(F32)
    outs = []
    for h in range(heads):
        log_sum = partial[:, :, heads * HD + 3 * h : heads * HD + 3 * h + 3]
        log_sum = jnp.sum(log_sum, axis=2, keepdims=True)
        scale = jnp.exp(log_sum - jnp.max(log_sum, axis=0, keepdims=True))
        acc = jnp.sum(scale * partial[:, :, h * HD : (h + 1) * HD], axis=0)
        outs.append(acc / jnp.sum(scale, axis=0))
    heads_out = jnp.concatenate(outs, 1).astype(BF16)

    projected = jnp.dot(heads_out, w_out, preferred_element_type=F32).astype(BF16)
    projected = exchange(projected.reshape(2 * TP, own_rows, width), GROUP)
    attention = jnp.sum(projected.astype(F32), axis=0)
    own_tokens = lax.dynamic_slice_in_dim(tokens, group * own_rows, own_rows, 0).astype(F32)
    resid = own_tokens + modulation[0] * attention
    row_mean = jnp.mean(resid, axis=1, keepdims=True)
    row_square = jnp.mean(resid * resid, axis=1, keepdims=True)
    inv_dev = lax.rsqrt(row_square - row_mean * row_mean + 1e-06)
    normed = ((resid - row_mean) * inv_dev * (1.0 + modulation[2]) + modulation[1]).astype(BF16)

    own_ids = lax.dynamic_slice_in_dim(expert_ids, group * own_rows, own_rows, 0)
    own_gates = lax.dynamic_slice_in_dim(gate_values, group * own_rows, own_rows, 0)
    gates_hi = lax.reduce_precision(own_gates, 8, 7)
    gates_lo = own_gates - gates_hi
    route = jnp.concatenate(
        [own_ids.astype(BF16), gates_hi.astype(BF16), gates_lo.astype(BF16)], 1
    )
    route = jnp.pad(route, ((0, 0), (0, HD - route.shape[1])))
    sent = jnp.concatenate([normed, route], 1)
    ring = spread(sent, "z", Z).reshape(Z * own_rows, width + HD)
    mine, ring = lax.optimization_barrier((mine, ring))
    other = lax.ppermute(mine, "pool", [(0, 1), (1, 0)])
    rows_in = spread(ring, "tp", TP).reshape(TP * Z * own_rows, width + HD)
    ids = jnp.stack([group, (1 - pool) * TP + tp]).astype(jnp.int32)
    mixed = ffn(ids, rows_in, mine, other)

    mixed = exchange(mixed.reshape(TP, Z * own_rows, width), "tp")
    mixed = jnp.sum(mixed.astype(F32), axis=0).astype(BF16)
    mixed = exchange(mixed.reshape(Z, own_rows, width), "z")
    mixture = jnp.sum(mixed.astype(F32), axis=0)
    block_out = (resid + modulation[3] * mixture).astype(BF16)
    block_out = block_out.reshape(own_rows, 2 * TP, width // (2 * TP)).transpose(1, 0, 2)
    return exchange(block_out, GROUP).reshape(rows, width // (2 * TP))


def solution(mesh):
    split = Mesh(
        mesh.devices.reshape(2, Y, Z, TP), ("pool", "y", "z", "tp")
    )
    seq = ("y", "z")
    in_specs = (
        P(seq, None),
        P(seq, GROUP),
        P(seq, GROUP),
        P(seq, GROUP),
        P(GROUP, None),
        P(),
        P(seq, None),
        P(seq, None),
        P(GROUP, None, seq),
        P(GROUP, None, seq),
        P(GROUP, seq, None),
    )
    return jax.shard_map(
        body, mesh=split, in_specs=in_specs, out_specs=P(seq, GROUP), check_vma=False
    )
```

```python
import math

import jax
import jax.numpy as jnp
from jax import lax
from jax.experimental import pallas as pl
from jax.experimental.pallas import tpu as pltpu
from jax.sharding import Mesh
from jax.sharding import PartitionSpec as P

HD = 128
Y = 4
Z = 16
TP = 4
GROUP = ("pool", "tp")
F32 = jnp.float32
BF16 = jnp.bfloat16


def copies_of(x, count):
    return jnp.broadcast_to(x[None], (count,) + x.shape)


def spread(x, axis, count):
    return exchange(copies_of(x, count), axis)


def shift(x, axis, count):
    size = lax.axis_size(axis)
    return lax.ppermute(x, axis, [(i, (i + count) % size) for i in range(size)])


def exchange(x, axis):
    return lax.all_to_all(x, axis, split_axis=0, concat_axis=0, tiled=True)


def pack_weights(w_gate, w_up, w_down):
    pad = -w_down.shape[0] % 16
    return jnp.concatenate(
        [jnp.pad(w, ((0, pad), (0, 0))) for w in (w_gate.T, w_up.T, w_down)], 0
    )


def ffn_kernel(ids_ref, x_ref, mine_ref, other_ref, o_ref, xt_ref, act_ref, down_ref):
    step = pl.program_id(0)
    width = o_ref.shape[1]
    hidden = mine_ref.shape[1] // 3
    weights = [
        (e, w, s) for s in range(mine_ref.shape[0]) for e, w in enumerate((mine_ref, other_ref))
    ]

    @pl.when(step == 0)
    def _():
        xt_ref[...] = x_ref[...].T

    route = xt_ref[width : width + 16].astype(F32)
    scales = []
    for e in range(2):
        scale = jnp.zeros((1, x_ref.shape[0]), F32)
        for k in range(2):
            value = route[2 + k : 3 + k] + route[4 + k : 5 + k]
            scale += jnp.where(route[k : k + 1] == ids_ref[e].astype(F32), value, 0.0)
        scales.append(scale)
    both = jnp.dot(
        jnp.concatenate([w[s, : 2 * hidden] for _, w, s in weights], 0),
        xt_ref[:width],
        preferred_element_type=F32,
    )
    acts = []
    for i, (e, _, _) in enumerate(weights):
        gate = both[2 * i * hidden : (2 * i + 1) * hidden]
        up = both[(2 * i + 1) * hidden : (2 * i + 2) * hidden]
        acts.append((gate / (1.0 + jnp.exp(-gate)) * up * scales[e]).astype(BF16))
    units = len(weights) * hidden
    here = pl.ds(pl.multiple_of(step * units, 16), units)
    act_ref[here] = jnp.concatenate(acts, 0)
    down_ref[here] = jnp.concatenate([w[s, 2 * hidden :] for _, w, s in weights], 0)

    @pl.when(step == pl.num_programs(0) - 1)
    def _():
        o_ref[...] = lax.dot_general(
            act_ref[...], down_ref[...], (((0,), (0,)), ((), ())), preferred_element_type=F32
        ).astype(BF16)


def ffn(ids, x, mine, other):
    rows = x.shape[0]
    parts, depth, width = mine.shape
    each = 2
    units = 2 * parts * (depth // 3)
    weights = pl.BlockSpec((each, depth, width), lambda i: (i, 0, 0))
    return pl.pallas_call(
        ffn_kernel,
        grid=(parts // each,),
        out_shape=jax.ShapeDtypeStruct((rows, width), BF16),
        in_specs=[
            pl.BlockSpec(memory_space=pltpu.SMEM),
            pl.BlockSpec(x.shape, lambda i: (0, 0)),
            weights,
            weights,
        ],
        out_specs=pl.BlockSpec((rows, width), lambda i: (0, 0)),
        scratch_shapes=[
            pltpu.VMEM((x.shape[1], rows), BF16),
            pltpu.VMEM((units, rows), BF16),
            pltpu.VMEM((units, width), BF16),
        ],
        compiler_params=pltpu.CompilerParams(vmem_limit_bytes=58 << 20),
        cost_estimate=pl.CostEstimate(
            flops=4 * rows * width * depth * parts,
            bytes_accessed=4 * width * depth * parts,
            transcendentals=0,
        ),
    )(ids, x, mine, other)


def body(
    tokens,
    query_proj,
    key_proj,
    value_proj,
    w_out,
    modulation,
    expert_ids,
    gate_values,
    w_gate,
    w_up,
    w_down,
):
    rows, width = tokens.shape
    heads = query_proj.shape[1] // HD
    own_rows = rows // (2 * TP)
    pool = lax.axis_index("pool")
    tp = lax.axis_index("tp")
    group = pool * TP + tp

    key_value = spread(jnp.concatenate([key_proj, value_proj], 1), "z", Z)
    key_value = key_value.reshape(Z * rows, 2 * heads * HD)
    blocks = [query_proj] + [shift(query_proj, "y", -k) for k in range(1, Y)]
    first = (Y - lax.axis_index("y")) % Y * rows
    queries = lax.dynamic_slice_in_dim(
        jnp.concatenate(blocks + blocks[: Y - 1], 0), first, Y * rows, 0
    )

    w_gate, w_up, w_down, queries = lax.optimization_barrier((w_gate, w_up, w_down, queries))
    packed = pack_weights(w_gate[0], w_up[0], w_down[0])
    before = shift(packed, "y", 1)
    after = shift(packed, "y", -1)

    parts = []
    stats = []
    for h in range(heads):
        cols = slice(h * HD, (h + 1) * HD)
        keys = key_value[:, cols]
        values = key_value[:, heads * HD + h * HD : heads * HD + (h + 1) * HD]
        scores = lax.dot_general(
            queries[:, cols], keys, (((1,), (1,)), ((), ())), preferred_element_type=F32
        ) * (1.0 / math.sqrt(HD))
        top = jnp.max(scores, axis=1, keepdims=True)
        weights = jnp.exp(scores - top)
        total = jnp.sum(weights, axis=1, keepdims=True)
        part = jnp.dot(weights.astype(BF16), values, preferred_element_type=F32)
        parts.append((part / total).astype(BF16))
        log_sum = top + jnp.log(total)
        high = lax.reduce_precision(log_sum, 8, 7)
        middle = lax.reduce_precision(log_sum - high, 8, 7)
        stats += [high, middle, log_sum - high - middle]
    stats = jnp.concatenate(stats, 1).astype(BF16)
    stats = jnp.pad(stats, ((0, 0), (0, HD - stats.shape[1])))
    partial = jnp.concatenate(parts + [stats], 1).reshape(Y, rows, (heads + 1) * HD)
    partial = exchange(partial, "y").astype(F32)
    outs = []
    for h in range(heads):
        log_sum = partial[:, :, heads * HD + 3 * h : heads * HD + 3 * h + 3]
        log_sum = jnp.sum(log_sum, axis=2, keepdims=True)
        scale = jnp.exp(log_sum - jnp.max(log_sum, axis=0, keepdims=True))
        acc = jnp.sum(scale * partial[:, :, h * HD : (h + 1) * HD], axis=0)
        outs.append(acc / jnp.sum(scale, axis=0))
    heads_out = jnp.concatenate(outs, 1).astype(BF16)

    projected = jnp.dot(heads_out, w_out, preferred_element_type=F32).astype(BF16)
    projected = projected.reshape(2 * TP, own_rows, width)
    before, after, projected = lax.optimization_barrier((before, after, projected))
    split = packed.shape[0] * 2 // 3
    across = [shift(before[:split], "y", 1), shift(after[split:], "y", -1)]
    projected = exchange(projected, GROUP)
    attention = jnp.sum(projected.astype(F32), axis=0)
    own_tokens = lax.dynamic_slice_in_dim(tokens, group * own_rows, own_rows, 0).astype(F32)
    resid = own_tokens + modulation[0] * attention
    row_mean = jnp.mean(resid, axis=1, keepdims=True)
    row_square = jnp.mean(resid * resid, axis=1, keepdims=True)
    inv_dev = lax.rsqrt(row_square - row_mean * row_mean + 1e-06)
    normed = ((resid - row_mean) * inv_dev * (1.0 + modulation[2]) + modulation[1]).astype(BF16)

    own_ids = lax.dynamic_slice_in_dim(expert_ids, group * own_rows, own_rows, 0)
    own_gates = lax.dynamic_slice_in_dim(gate_values, group * own_rows, own_rows, 0)
    gates_hi = lax.reduce_precision(own_gates, 8, 7)
    gates_lo = own_gates - gates_hi
    route = jnp.concatenate(
        [own_ids.astype(BF16), gates_hi.astype(BF16), gates_lo.astype(BF16)], 1
    )
    route = jnp.pad(route, ((0, 0), (0, HD - route.shape[1])))
    sent = jnp.concatenate([normed, route], 1)
    copies = copies_of(exchange(copies_of(sent, Z), "z").reshape(Z * own_rows, width + HD), TP)
    packed, before, after, *across, copies = lax.optimization_barrier(
        (packed, before, after, *across, copies)
    )
    mine = jnp.concatenate([packed, before, after, *across], 0).reshape(Y, -1, width)
    other = lax.ppermute(mine, "pool", [(0, 1), (1, 0)])
    rows_in = exchange(copies, "tp").reshape(TP * Z * own_rows, width + HD)
    ids = jnp.stack([group, (1 - pool) * TP + tp]).astype(jnp.int32)
    mixed = ffn(ids, rows_in, mine, other)

    mixed = exchange(mixed.reshape(TP, Z * own_rows, width), "tp")
    mixed = jnp.sum(mixed.astype(F32), axis=0).astype(BF16)
    mixed = exchange(mixed.reshape(Z, own_rows, width), "z")
    mixture = jnp.sum(mixed.astype(F32), axis=0)
    block_out = (resid + modulation[3] * mixture).astype(BF16)
    block_out = block_out.reshape(own_rows, 2 * TP, width // (2 * TP)).transpose(1, 0, 2)
    return exchange(block_out, GROUP).reshape(rows, width // (2 * TP))


def solution(mesh):
    split = Mesh(
        mesh.devices.reshape(2, Y, Z, TP), ("pool", "y", "z", "tp")
    )
    seq = ("y", "z")
    in_specs = (
        P(seq, None),
        P(seq, GROUP),
        P(seq, GROUP),
        P(seq, GROUP),
        P(GROUP, None),
        P(),
        P(seq, None),
        P(seq, None),
        P(GROUP, None, seq),
        P(GROUP, None, seq),
        P(GROUP, seq, None),
    )
    return jax.shard_map(
        body, mesh=split, in_specs=in_specs, out_specs=P(seq, GROUP), check_vma=False
    )
```

```python
import math

import jax
import jax.numpy as jnp
from jax import lax
from jax.experimental import pallas as pl
from jax.experimental.pallas import tpu as pltpu
from jax.sharding import Mesh
from jax.sharding import PartitionSpec as P

HD = 128
Y = 4
Z = 16
TP = 4
GROUP = ("pool", "tp")
F32 = jnp.float32
BF16 = jnp.bfloat16


def copies_of(x, count):
    return jnp.broadcast_to(x[None], (count,) + x.shape)


def spread(x, axis, count):
    return exchange(copies_of(x, count), axis)


def shift(x, axis, count):
    size = lax.axis_size(axis)
    return lax.ppermute(x, axis, [(i, (i + count) % size) for i in range(size)])


def swap(x):
    return lax.ppermute(x, "pool", [(0, 1), (1, 0)])


def exchange(x, axis):
    return lax.all_to_all(x, axis, split_axis=0, concat_axis=0, tiled=True)


def attention_kernel(q_ref, kv_ref, o_ref):
    heads = q_ref.shape[1] // HD
    lane = lax.broadcasted_iota(jnp.int32, (q_ref.shape[0], HD), 1)
    stats = jnp.zeros(lane.shape, F32)
    for h in range(heads):
        cols = slice(h * HD, (h + 1) * HD)
        values = kv_ref[:, (heads + h) * HD : (heads + h + 1) * HD]
        scores = lax.dot_general(
            q_ref[:, cols], kv_ref[:, cols], (((1,), (1,)), ((), ())), preferred_element_type=F32
        ) * (1.0 / math.sqrt(HD))
        top = jnp.max(scores, axis=1, keepdims=True)
        weights = jnp.exp(scores - top)
        total = jnp.sum(weights, axis=1, keepdims=True)
        part = jnp.dot(weights.astype(BF16), values, preferred_element_type=F32)
        o_ref[:, cols] = (part / total).astype(BF16)
        rest = top + jnp.log(total)
        for k in range(3):
            term = rest.astype(BF16).astype(F32)
            stats = jnp.where(lane == 3 * h + k, term, stats)
            rest = rest - term
    o_ref[:, heads * HD :] = stats.astype(BF16)


def attend(queries, key_value):
    rows, depth = queries.shape
    return pl.pallas_call(
        attention_kernel,
        out_shape=jax.ShapeDtypeStruct((rows, depth + HD), BF16),
        compiler_params=pltpu.CompilerParams(vmem_limit_bytes=16 << 20),
        cost_estimate=pl.CostEstimate(
            flops=4 * rows * depth * key_value.shape[0],
            bytes_accessed=2 * key_value.size,
            transcendentals=0,
        ),
    )(queries, key_value)


def project_kernel(partial_ref, w_ref, o_ref):
    heads = w_ref.shape[0] // HD
    outs = []
    for h in range(heads):
        first = heads * HD + 3 * h
        log_sums = []
        for y in range(Y):
            terms = partial_ref[y, :, heads * HD :].astype(F32)
            at = first - heads * HD
            log_sums.append(
                terms[:, at : at + 1] + terms[:, at + 1 : at + 2] + terms[:, at + 2 : at + 3]
            )
        top = log_sums[0]
        for y in range(1, Y):
            top = jnp.maximum(top, log_sums[y])
        acc = jnp.zeros((partial_ref.shape[1], HD), F32)
        total = jnp.zeros_like(top)
        for y in range(Y):
            scale = jnp.exp(log_sums[y] - top)
            total += scale
            acc += scale * partial_ref[y, :, h * HD : (h + 1) * HD].astype(F32)
        outs.append((acc / total).astype(BF16))
    o_ref[...] = jnp.dot(
        jnp.concatenate(outs, 1), w_ref[...], preferred_element_type=F32
    ).astype(BF16)


def project(partial, w_out):
    return pl.pallas_call(
        project_kernel,
        out_shape=jax.ShapeDtypeStruct((partial.shape[1], w_out.shape[1]), BF16),
        compiler_params=pltpu.CompilerParams(vmem_limit_bytes=16 << 20),
        cost_estimate=pl.CostEstimate(
            flops=2 * partial.shape[1] * w_out.size,
            bytes_accessed=2 * w_out.size,
            transcendentals=0,
        ),
    )(partial, w_out)


def pack_weights(w_gate, w_up, w_down):
    pad = -w_down.shape[0] % 16
    return jnp.concatenate(
        [jnp.pad(w, ((0, pad), (0, 0))) for w in (w_gate.T, w_up.T, w_down)], 0
    )


def ffn_kernel(ids_ref, x_hbm, *refs):
    parts = refs[: 2 * TP]
    o_ref, x_ref, w_ref, act_ref, down_ref, sems = refs[2 * TP :]
    width = o_ref.shape[1]
    hidden = w_ref.shape[1] // 3
    x_copy = pltpu.make_async_copy(x_hbm, x_ref, sems.at[2 * TP])
    x_copy.start()
    copies = []
    for i, part in enumerate(parts):
        copies.append(pltpu.make_async_copy(part, w_ref.at[i], sems.at[i]))
        copies[i].start()
    x_copy.wait()
    x = x_ref[:, :width]
    route = x_ref[:, width:].astype(F32).T
    scales = []
    for e in range(2 * TP):
        scale = jnp.zeros((1, x.shape[0]), F32)
        for k in range(2):
            value = route[2 + k : 3 + k] + route[4 + k : 5 + k]
            scale += jnp.where(route[k : k + 1] == ids_ref[e].astype(F32), value, 0.0)
        scales.append(scale)
    each = 4
    for first in range(0, 2 * TP, each):
        for i in range(first, first + each):
            copies[i].wait()
        both = lax.dot_general(
            jnp.concatenate([w_ref[i, : 2 * hidden] for i in range(first, first + each)], 0),
            x,
            (((1,), (1,)), ((), ())),
            preferred_element_type=F32,
        )
        for i in range(first, first + each):
            gate = both[2 * (i - first) * hidden : (2 * (i - first) + 1) * hidden]
            up = both[(2 * (i - first) + 1) * hidden : (2 * (i - first) + 2) * hidden]
            here = slice(i * hidden, (i + 1) * hidden)
            act = gate / (1.0 + jnp.exp(-gate)) * up * scales[i]
            act_ref[here] = act.astype(BF16)
            down_ref[here] = w_ref[i, 2 * hidden :]
    o_ref[...] = lax.dot_general(
        act_ref[...], down_ref[...], (((0,), (0,)), ((), ())), preferred_element_type=F32
    ).astype(BF16)


def ffn(ids, x, mine, other):
    rows = x.shape[0]
    depth, width = mine[0].shape
    units = 2 * TP * (depth // 3)
    return pl.pallas_call(
        ffn_kernel,
        out_shape=jax.ShapeDtypeStruct((rows, width), BF16),
        in_specs=[pl.BlockSpec(memory_space=pltpu.SMEM)]
        + [pl.BlockSpec(memory_space=pl.ANY)] * (1 + 2 * TP),
        out_specs=pl.BlockSpec(memory_space=pltpu.VMEM),
        scratch_shapes=[
            pltpu.VMEM(x.shape, BF16),
            pltpu.VMEM((2 * TP, depth, width), BF16),
            pltpu.VMEM((units, rows), BF16),
            pltpu.VMEM((units, width), BF16),
            pltpu.SemaphoreType.DMA((2 * TP + 1,)),
        ],
        compiler_params=pltpu.CompilerParams(vmem_limit_bytes=36 << 20),
        cost_estimate=pl.CostEstimate(
            flops=4 * rows * width * depth * TP,
            bytes_accessed=4 * width * depth * TP,
            transcendentals=0,
        ),
    )(ids, x, *mine, *other)


def body(
    tokens,
    query_proj,
    key_proj,
    value_proj,
    w_out,
    modulation,
    expert_ids,
    gate_values,
    w_gate,
    w_up,
    w_down,
):
    rows, width = tokens.shape
    heads = query_proj.shape[1] // HD
    own_rows = rows // (2 * TP)
    pool = lax.axis_index("pool")
    tp = lax.axis_index("tp")
    group = pool * TP + tp

    packed = pack_weights(w_gate[0], w_up[0], w_down[0])
    before = shift(packed, "tp", 1)
    after = shift(packed, "tp", -1)

    queries = spread(query_proj, "y", Y).reshape(Y * rows, heads * HD)
    queries, key_proj = lax.optimization_barrier((queries, key_proj))
    key_value = spread(jnp.concatenate([key_proj, value_proj], 1), "z", Z)
    key_value = key_value.reshape(Z * rows, 2 * heads * HD)
    partial = exchange(attend(queries, key_value).reshape(Y, rows, (heads + 1) * HD), "y")

    projected = project(partial, w_out).reshape(2 * TP, own_rows, width)
    before, after, projected = lax.optimization_barrier((before, after, projected))
    across = shift(before, "tp", 1)
    projected = exchange(projected, GROUP)
    attention = jnp.sum(projected.astype(F32), axis=0)
    own_tokens = lax.dynamic_slice_in_dim(tokens, group * own_rows, own_rows, 0).astype(F32)
    resid = own_tokens + modulation[0] * attention
    row_mean = jnp.mean(resid, axis=1, keepdims=True)
    row_square = jnp.mean(resid * resid, axis=1, keepdims=True)
    inv_dev = lax.rsqrt(row_square - row_mean * row_mean + 1e-06)
    normed = ((resid - row_mean) * inv_dev * (1.0 + modulation[2]) + modulation[1]).astype(BF16)

    own_ids = lax.dynamic_slice_in_dim(expert_ids, group * own_rows, own_rows, 0)
    own_gates = lax.dynamic_slice_in_dim(gate_values, group * own_rows, own_rows, 0)
    gates_hi = lax.reduce_precision(own_gates, 8, 7)
    gates_lo = own_gates - gates_hi
    route = jnp.concatenate(
        [own_ids.astype(BF16), gates_hi.astype(BF16), gates_lo.astype(BF16)], 1
    )
    route = jnp.pad(route, ((0, 0), (0, HD - route.shape[1])))
    sent = jnp.concatenate([normed, route], 1)
    copies = copies_of(sent, Z)
    packed, before, after, copies = lax.optimization_barrier((packed, before, after, copies))
    mine = [packed, before, after]
    other = [swap(w) for w in mine]
    copies = copies_of(exchange(copies, "z").reshape(Z * own_rows, width + HD), Y)
    across, copies = lax.optimization_barrier((across, copies))
    mine.append(across)
    other.append(swap(across))
    rows_in = exchange(copies, "y").reshape(Y * Z * own_rows, width + HD)
    near = (tp + jnp.array([0, TP - 1, 1, 2], jnp.int32)) % TP
    ids = jnp.concatenate([pool * TP + near, (1 - pool) * TP + near]).astype(jnp.int32)
    mixed = ffn(ids, rows_in, mine, other)

    mixed = exchange(mixed.reshape(Y, Z * own_rows, width), "y")
    mixed = jnp.sum(mixed.astype(F32), axis=0).astype(BF16)
    mixed = exchange(mixed.reshape(Z, own_rows, width), "z")
    mixture = jnp.sum(mixed.astype(F32), axis=0)
    block_out = (resid + modulation[3] * mixture).astype(BF16)
    block_out = block_out.reshape(own_rows, 2 * TP, width // (2 * TP)).transpose(1, 0, 2)
    return exchange(block_out, GROUP).reshape(rows, width // (2 * TP))


def solution(mesh):
    split = Mesh(
        mesh.devices.reshape(2, Y, Z, TP), ("pool", "y", "z", "tp")
    )
    seq = ("y", "z")
    in_specs = (
        P(seq, None),
        P(seq, GROUP),
        P(seq, GROUP),
        P(seq, GROUP),
        P(GROUP, None),
        P(),
        P(seq, None),
        P(seq, None),
        P(GROUP, None, seq),
        P(GROUP, None, seq),
        P(GROUP, seq, None),
    )
    return jax.shard_map(
        body, mesh=split, in_specs=in_specs, out_specs=P(seq, GROUP), check_vma=False
    )
```

```python
import math

import jax
import jax.numpy as jnp
from jax import lax
from jax.experimental import pallas as pl
from jax.experimental.pallas import tpu as pltpu
from jax.sharding import Mesh
from jax.sharding import PartitionSpec as P

HD = 128
Y = 4
Z = 16
TP = 4
GROUP = ("pool", "tp")
F32 = jnp.float32
BF16 = jnp.bfloat16


def copies_of(x, count):
    return jnp.broadcast_to(x[None], (count,) + x.shape)


def spread(x, axis, count):
    return exchange(copies_of(x, count), axis)


def shift(x, axis, count):
    size = lax.axis_size(axis)
    return lax.ppermute(x, axis, [(i, (i + count) % size) for i in range(size)])


def swap(x):
    return lax.ppermute(x, "pool", [(0, 1), (1, 0)])


def exchange(x, axis):
    return lax.all_to_all(x, axis, split_axis=0, concat_axis=0, tiled=True)


def attention_kernel(q_ref, kv_ref, o_ref):
    heads = q_ref.shape[1] // HD
    lane = lax.broadcasted_iota(jnp.int32, (q_ref.shape[0], HD), 1)
    stats = jnp.zeros(lane.shape, F32)
    for h in range(heads):
        cols = slice(h * HD, (h + 1) * HD)
        values = kv_ref[:, (heads + h) * HD : (heads + h + 1) * HD]
        scores = lax.dot_general(
            q_ref[:, cols], kv_ref[:, cols], (((1,), (1,)), ((), ())), preferred_element_type=F32
        ) * (1.0 / math.sqrt(HD))
        top = jnp.max(scores, axis=1, keepdims=True)
        weights = jnp.exp(scores - top)
        total = jnp.sum(weights, axis=1, keepdims=True)
        part = jnp.dot(weights.astype(BF16), values, preferred_element_type=F32)
        o_ref[:, cols] = (part / total).astype(BF16)
        rest = top + jnp.log(total)
        for k in range(3):
            term = rest.astype(BF16).astype(F32)
            stats = jnp.where(lane == 3 * h + k, term, stats)
            rest = rest - term
    o_ref[:, heads * HD :] = stats.astype(BF16)


def attend(queries, key_value):
    rows, depth = queries.shape
    return pl.pallas_call(
        attention_kernel,
        out_shape=jax.ShapeDtypeStruct((rows, depth + HD), BF16),
        compiler_params=pltpu.CompilerParams(vmem_limit_bytes=16 << 20),
        cost_estimate=pl.CostEstimate(
            flops=4 * rows * depth * key_value.shape[0],
            bytes_accessed=2 * key_value.size,
            transcendentals=0,
        ),
    )(queries, key_value)


def pack_weights(w_gate, w_up, w_down):
    pad = -w_down.shape[0] % 16
    return jnp.concatenate(
        [jnp.pad(w, ((0, pad), (0, 0))) for w in (w_gate.T, w_up.T, w_down)], 0
    )


def ffn_kernel(ids_ref, x_hbm, *refs):
    parts = refs[: 2 * TP]
    o_ref, x_ref, w_ref, act_ref, down_ref, sems = refs[2 * TP :]
    width = o_ref.shape[1]
    hidden = w_ref.shape[1] // 3
    x_copy = pltpu.make_async_copy(x_hbm, x_ref, sems.at[2 * TP])
    x_copy.start()
    copies = []
    for i, part in enumerate(parts):
        copies.append(pltpu.make_async_copy(part, w_ref.at[i], sems.at[i]))
        copies[i].start()
    x_copy.wait()
    x = x_ref[:, :width]
    route = x_ref[:, width:].astype(F32).T
    scales = []
    for e in range(2 * TP):
        scale = jnp.zeros((1, x.shape[0]), F32)
        for k in range(2):
            value = route[2 + k : 3 + k] + route[4 + k : 5 + k]
            scale += jnp.where(route[k : k + 1] == ids_ref[e].astype(F32), value, 0.0)
        scales.append(scale)
    each = 4
    for first in range(0, 2 * TP, each):
        for i in range(first, first + each):
            copies[i].wait()
        both = lax.dot_general(
            jnp.concatenate([w_ref[i, : 2 * hidden] for i in range(first, first + each)], 0),
            x,
            (((1,), (1,)), ((), ())),
            preferred_element_type=F32,
        )
        for i in range(first, first + each):
            gate = both[2 * (i - first) * hidden : (2 * (i - first) + 1) * hidden]
            up = both[(2 * (i - first) + 1) * hidden : (2 * (i - first) + 2) * hidden]
            here = slice(i * hidden, (i + 1) * hidden)
            act = gate / (1.0 + jnp.exp(-gate)) * up * scales[i]
            act_ref[here] = act.astype(BF16)
            down_ref[here] = w_ref[i, 2 * hidden :]
    o_ref[...] = lax.dot_general(
        act_ref[...], down_ref[...], (((0,), (0,)), ((), ())), preferred_element_type=F32
    ).astype(BF16)


def ffn(ids, x, mine, other):
    rows = x.shape[0]
    depth, width = mine[0].shape
    units = 2 * TP * (depth // 3)
    return pl.pallas_call(
        ffn_kernel,
        out_shape=jax.ShapeDtypeStruct((rows, width), BF16),
        in_specs=[pl.BlockSpec(memory_space=pltpu.SMEM)]
        + [pl.BlockSpec(memory_space=pl.ANY)] * (1 + 2 * TP),
        out_specs=pl.BlockSpec(memory_space=pltpu.VMEM),
        scratch_shapes=[
            pltpu.VMEM(x.shape, BF16),
            pltpu.VMEM((2 * TP, depth, width), BF16),
            pltpu.VMEM((units, rows), BF16),
            pltpu.VMEM((units, width), BF16),
            pltpu.SemaphoreType.DMA((2 * TP + 1,)),
        ],
        compiler_params=pltpu.CompilerParams(vmem_limit_bytes=36 << 20),
        cost_estimate=pl.CostEstimate(
            flops=4 * rows * width * depth * TP,
            bytes_accessed=4 * width * depth * TP,
            transcendentals=0,
        ),
    )(ids, x, *mine, *other)


def body(
    tokens,
    query_proj,
    key_proj,
    value_proj,
    w_out,
    modulation,
    expert_ids,
    gate_values,
    w_gate,
    w_up,
    w_down,
):
    rows, width = tokens.shape
    heads = query_proj.shape[1] // HD
    own_rows = rows // (2 * TP)
    pool = lax.axis_index("pool")
    tp = lax.axis_index("tp")
    group = pool * TP + tp

    packed = pack_weights(w_gate[0], w_up[0], w_down[0])
    before = shift(packed, "tp", 1)
    after = shift(packed, "tp", -1)

    queries = spread(query_proj, "y", Y).reshape(Y * rows, heads * HD)
    key_value = lax.all_gather(
        jnp.concatenate([key_proj, value_proj], 1), "z", axis=0, tiled=True
    )
    partial = attend(queries, key_value)

    packed, before, after, partial = lax.optimization_barrier((packed, before, after, partial))
    mine = [packed, before, after]
    other = [swap(w) for w in mine]
    partial = exchange(partial.reshape(Y, rows, (heads + 1) * HD), "y").astype(F32)
    outs = []
    for h in range(heads):
        log_sum = partial[:, :, heads * HD + 3 * h : heads * HD + 3 * h + 3]
        log_sum = jnp.sum(log_sum, axis=2, keepdims=True)
        scale = jnp.exp(log_sum - jnp.max(log_sum, axis=0, keepdims=True))
        acc = jnp.sum(scale * partial[:, :, h * HD : (h + 1) * HD], axis=0)
        outs.append(acc / jnp.sum(scale, axis=0))
    heads_out = jnp.concatenate(outs, 1).astype(BF16)

    projected = jnp.dot(heads_out, w_out, preferred_element_type=F32).astype(BF16)
    projected = projected.reshape(2 * TP, own_rows, width)
    before, projected, *other = lax.optimization_barrier((before, projected, *other))
    across = shift(before, "tp", 1)
    projected = exchange(projected, GROUP)
    attention = jnp.sum(projected.astype(F32), axis=0)
    own_tokens = lax.dynamic_slice_in_dim(tokens, group * own_rows, own_rows, 0).astype(F32)
    resid = own_tokens + modulation[0] * attention
    row_mean = jnp.mean(resid, axis=1, keepdims=True)
    row_square = jnp.mean(resid * resid, axis=1, keepdims=True)
    inv_dev = lax.rsqrt(row_square - row_mean * row_mean + 1e-06)
    normed = ((resid - row_mean) * inv_dev * (1.0 + modulation[2]) + modulation[1]).astype(BF16)

    own_ids = lax.dynamic_slice_in_dim(expert_ids, group * own_rows, own_rows, 0)
    own_gates = lax.dynamic_slice_in_dim(gate_values, group * own_rows, own_rows, 0)
    gates_hi = lax.reduce_precision(own_gates, 8, 7)
    gates_lo = own_gates - gates_hi
    route = jnp.concatenate(
        [own_ids.astype(BF16), gates_hi.astype(BF16), gates_lo.astype(BF16)], 1
    )
    route = jnp.pad(route, ((0, 0), (0, HD - route.shape[1])))
    sent = jnp.concatenate([normed, route], 1)
    copies = copies_of(sent, Z)
    copies = copies_of(exchange(copies, "z").reshape(Z * own_rows, width + HD), Y)
    across, copies = lax.optimization_barrier((across, copies))
    mine.append(across)
    other.append(swap(across))
    rows_in = exchange(copies, "y").reshape(Y * Z * own_rows, width + HD)
    near = (tp + jnp.array([0, TP - 1, 1, 2], jnp.int32)) % TP
    ids = jnp.concatenate([pool * TP + near, (1 - pool) * TP + near]).astype(jnp.int32)
    mixed = ffn(ids, rows_in, mine, other)

    mixed = exchange(mixed.reshape(Y, Z * own_rows, width), "y")
    mixed = jnp.sum(mixed.astype(F32), axis=0).astype(BF16)
    mixed = exchange(mixed.reshape(Z, own_rows, width), "z")
    mixture = jnp.sum(mixed.astype(F32), axis=0)
    block_out = (resid + modulation[3] * mixture).astype(BF16)
    block_out = block_out.reshape(own_rows, 2 * TP, width // (2 * TP)).transpose(1, 0, 2)
    return exchange(block_out, GROUP).reshape(rows, width // (2 * TP))


def solution(mesh):
    split = Mesh(
        mesh.devices.reshape(2, Y, Z, TP), ("pool", "y", "z", "tp")
    )
    seq = ("y", "z")
    in_specs = (
        P(seq, None),
        P(seq, GROUP),
        P(seq, GROUP),
        P(seq, GROUP),
        P(GROUP, None),
        P(),
        P(seq, None),
        P(seq, None),
        P(GROUP, None, seq),
        P(GROUP, None, seq),
        P(GROUP, seq, None),
    )
    return jax.shard_map(
        body, mesh=split, in_specs=in_specs, out_specs=P(seq, GROUP), check_vma=False
    )
```

```python
import functools
import math

import jax
import jax.numpy as jnp
from jax import lax
from jax.experimental import pallas as pl
from jax.experimental.pallas import tpu as pltpu
from jax.sharding import Mesh
from jax.sharding import PartitionSpec as P

HD = 128
Y = 4
Z = 16
TP = 4
GROUP = ("pool", "tp")
F32 = jnp.float32
BF16 = jnp.bfloat16


def copies_of(x, count):
    return jnp.broadcast_to(x[None], (count,) + x.shape)


def spread(x, axis, count):
    return exchange(copies_of(x, count), axis)


def shift(x, axis, count):
    size = lax.axis_size(axis)
    return lax.ppermute(x, axis, [(i, (i + count) % size) for i in range(size)])


def swap(x):
    return lax.ppermute(x, "pool", [(0, 1), (1, 0)])


def exchange(x, axis):
    return lax.all_to_all(x, axis, split_axis=0, concat_axis=0, tiled=True)


def attention_kernel(q_ref, kv_ref, o_ref):
    heads = q_ref.shape[1] // HD
    lane = lax.broadcasted_iota(jnp.int32, (q_ref.shape[0], HD), 1)
    stats = jnp.zeros(lane.shape, F32)
    for h in range(heads):
        cols = slice(h * HD, (h + 1) * HD)
        values = kv_ref[:, (heads + h) * HD : (heads + h + 1) * HD]
        scores = lax.dot_general(
            q_ref[:, cols], kv_ref[:, cols], (((1,), (1,)), ((), ())), preferred_element_type=F32
        ) * (1.0 / math.sqrt(HD))
        top = jnp.max(scores, axis=1, keepdims=True)
        weights = jnp.exp(scores - top)
        total = jnp.sum(weights, axis=1, keepdims=True)
        part = jnp.dot(weights.astype(BF16), values, preferred_element_type=F32)
        o_ref[:, cols] = (part / total).astype(BF16)
        rest = top + jnp.log(total)
        for k in range(3):
            term = rest.astype(BF16).astype(F32)
            stats = jnp.where(lane == 3 * h + k, term, stats)
            rest = rest - term
    o_ref[:, heads * HD :] = stats.astype(BF16)


def attend(queries, key_value):
    rows, depth = queries.shape
    return pl.pallas_call(
        attention_kernel,
        out_shape=jax.ShapeDtypeStruct((rows, depth + HD), BF16),
        compiler_params=pltpu.CompilerParams(vmem_limit_bytes=16 << 20),
        cost_estimate=pl.CostEstimate(
            flops=4 * rows * depth * key_value.shape[0],
            bytes_accessed=2 * key_value.size,
            transcendentals=0,
        ),
    )(queries, key_value)


def pack_weights(w_gate, w_up, w_down):
    pad = -w_down.shape[0] % 16
    return jnp.concatenate(
        [jnp.pad(w, ((0, pad), (0, 0))) for w in (w_gate.T, w_up.T, w_down)], 0
    )


def ffn_kernel(count, ids_ref, x_hbm, *refs):
    parts = refs[:count]
    sums = refs[count : len(refs) - 6]
    o_ref, x_ref, w_ref, act_ref, down_ref, sems = refs[len(refs) - 6 :]
    width = o_ref.shape[1]
    hidden = w_ref.shape[1] // 3
    x_copy = pltpu.make_async_copy(x_hbm, x_ref, sems.at[count])
    x_copy.start()
    copies = []
    for i, part in enumerate(parts):
        copies.append(pltpu.make_async_copy(part, w_ref.at[i], sems.at[i]))
        copies[i].start()
    x_copy.wait()
    x = x_ref[:, :width]
    route = x_ref[:, width:].astype(F32).T
    each = 3
    for first in range(0, count, each):
        group = range(first, min(first + each, count))
        for i in group:
            copies[i].wait()
        both = lax.dot_general(
            jnp.concatenate([w_ref[i, : 2 * hidden] for i in group], 0),
            x,
            (((1,), (1,)), ((), ())),
            preferred_element_type=F32,
        )
        for i in group:
            scale = jnp.zeros((1, x.shape[0]), F32)
            for k in range(2):
                value = route[2 + k : 3 + k] + route[4 + k : 5 + k]
                scale += jnp.where(route[k : k + 1] == ids_ref[i].astype(F32), value, 0.0)
            gate = both[2 * (i - first) * hidden : (2 * (i - first) + 1) * hidden]
            up = both[(2 * (i - first) + 1) * hidden : (2 * (i - first) + 2) * hidden]
            here = slice(i * hidden, (i + 1) * hidden)
            act_ref[here] = (gate / (1.0 + jnp.exp(-gate)) * up * scale).astype(BF16)
            down_ref[here] = w_ref[i, 2 * hidden :]
    out = lax.dot_general(
        act_ref[...], down_ref[...], (((0,), (0,)), ((), ())), preferred_element_type=F32
    )
    for so_far in sums:
        out += so_far[...]
    o_ref[...] = out.astype(o_ref.dtype)


def ffn(ids, x, parts, sums, dtype):
    rows = x.shape[0]
    count = len(parts)
    depth, width = parts[0].shape
    units = count * (depth // 3)
    vmem = pl.BlockSpec(memory_space=pltpu.VMEM)
    return pl.pallas_call(
        functools.partial(ffn_kernel, count),
        out_shape=jax.ShapeDtypeStruct((rows, width), dtype),
        in_specs=[pl.BlockSpec(memory_space=pltpu.SMEM)]
        + [pl.BlockSpec(memory_space=pl.ANY)] * (1 + count)
        + [vmem] * len(sums),
        out_specs=vmem,
        scratch_shapes=[
            pltpu.VMEM(x.shape, BF16),
            pltpu.VMEM((count, depth, width), BF16),
            pltpu.VMEM((units, rows), BF16),
            pltpu.VMEM((units, width), BF16),
            pltpu.SemaphoreType.DMA((count + 1,)),
        ],
        compiler_params=pltpu.CompilerParams(vmem_limit_bytes=30 << 20),
        cost_estimate=pl.CostEstimate(
            flops=16 * rows * width * depth * count,
            bytes_accessed=16 * width * depth * count,
            transcendentals=0,
        ),
    )(ids, x, *parts, *sums)


def body(
    tokens,
    query_proj,
    key_proj,
    value_proj,
    w_out,
    modulation,
    expert_ids,
    gate_values,
    w_gate,
    w_up,
    w_down,
):
    rows, width = tokens.shape
    heads = query_proj.shape[1] // HD
    own_rows = rows // (2 * TP)
    pool = lax.axis_index("pool")
    tp = lax.axis_index("tp")
    group = pool * TP + tp

    packed = pack_weights(w_gate[0], w_up[0], w_down[0])
    before = shift(packed, "tp", 1)
    after = shift(packed, "tp", -1)

    queries = spread(query_proj, "y", Y).reshape(Y * rows, heads * HD)
    key_value = lax.all_gather(
        jnp.concatenate([key_proj, value_proj], 1), "z", axis=0, tiled=True
    )
    partial = attend(queries, key_value)

    before, after, partial = lax.optimization_barrier((before, after, partial))
    across = shift(before, "tp", 1)
    partial = exchange(partial.reshape(Y, rows, (heads + 1) * HD), "y").astype(F32)
    outs = []
    for h in range(heads):
        log_sum = partial[:, :, heads * HD + 3 * h : heads * HD + 3 * h + 3]
        log_sum = jnp.sum(log_sum, axis=2, keepdims=True)
        scale = jnp.exp(log_sum - jnp.max(log_sum, axis=0, keepdims=True))
        acc = jnp.sum(scale * partial[:, :, h * HD : (h + 1) * HD], axis=0)
        outs.append(acc / jnp.sum(scale, axis=0))
    heads_out = jnp.concatenate(outs, 1).astype(BF16)

    projected = jnp.dot(heads_out, w_out, preferred_element_type=F32).astype(BF16)
    projected = projected.reshape(2 * TP, own_rows, width)
    projected = exchange(projected, GROUP)
    attention = jnp.sum(projected.astype(F32), axis=0)
    own_tokens = lax.dynamic_slice_in_dim(tokens, group * own_rows, own_rows, 0).astype(F32)
    resid = own_tokens + modulation[0] * attention
    row_mean = jnp.mean(resid, axis=1, keepdims=True)
    row_square = jnp.mean(resid * resid, axis=1, keepdims=True)
    inv_dev = lax.rsqrt(row_square - row_mean * row_mean + 1e-06)
    normed = ((resid - row_mean) * inv_dev * (1.0 + modulation[2]) + modulation[1]).astype(BF16)

    own_ids = lax.dynamic_slice_in_dim(expert_ids, group * own_rows, own_rows, 0)
    own_gates = lax.dynamic_slice_in_dim(gate_values, group * own_rows, own_rows, 0)
    gates_hi = lax.reduce_precision(own_gates, 8, 7)
    gates_lo = own_gates - gates_hi
    route = jnp.concatenate(
        [own_ids.astype(BF16), gates_hi.astype(BF16), gates_lo.astype(BF16)], 1
    )
    route = jnp.pad(route, ((0, 0), (0, HD - route.shape[1])))
    sent = jnp.concatenate([normed, route], 1)
    copies = copies_of(sent, Z)
    copies = copies_of(exchange(copies, "z").reshape(Z * own_rows, width + HD), Y)
    packed, before, after, copies = lax.optimization_barrier((packed, before, after, copies))
    early = [packed, before, after]
    across_tied, _ = lax.optimization_barrier((across, copies))
    late = [across] + [swap(w) for w in early + [across_tied]]
    rows_in = exchange(copies, "y").reshape(Y * Z * own_rows, width + HD)
    near = (tp + jnp.array([0, TP - 1, 1, 2], jnp.int32)) % TP
    ids = jnp.concatenate([pool * TP + near, (1 - pool) * TP + near]).astype(jnp.int32)
    mixed = ffn(ids[:3], rows_in, early, [], F32)
    mixed = ffn(ids[3:], rows_in, late, [mixed], BF16)

    mixed = exchange(mixed.reshape(Y, Z * own_rows, width), "y")
    mixed = jnp.sum(mixed.astype(F32), axis=0).astype(BF16)
    mixed = exchange(mixed.reshape(Z, own_rows, width), "z")
    mixture = jnp.sum(mixed.astype(F32), axis=0)
    block_out = (resid + modulation[3] * mixture).astype(BF16)
    block_out = block_out.reshape(own_rows, 2 * TP, width // (2 * TP)).transpose(1, 0, 2)
    return exchange(block_out, GROUP).reshape(rows, width // (2 * TP))


def solution(mesh):
    split = Mesh(
        mesh.devices.reshape(2, Y, Z, TP), ("pool", "y", "z", "tp")
    )
    seq = ("y", "z")
    in_specs = (
        P(seq, None),
        P(seq, GROUP),
        P(seq, GROUP),
        P(seq, GROUP),
        P(GROUP, None),
        P(),
        P(seq, None),
        P(seq, None),
        P(GROUP, None, seq),
        P(GROUP, None, seq),
        P(GROUP, seq, None),
    )
    return jax.shard_map(
        body, mesh=split, in_specs=in_specs, out_specs=P(seq, GROUP), check_vma=False
    )
```

```python
import functools
import math

import jax
import jax.numpy as jnp
from jax import lax
from jax.experimental import pallas as pl
from jax.experimental.pallas import tpu as pltpu
from jax.sharding import Mesh
from jax.sharding import PartitionSpec as P

HD = 128
Y = 4
Z = 16
TP = 4
GROUP = ("pool", "tp")
F32 = jnp.float32
BF16 = jnp.bfloat16


def copies_of(x, count):
    return jnp.broadcast_to(x[None], (count,) + x.shape)


def spread(x, axis, count):
    return exchange(copies_of(x, count), axis)


def shift(x, axis, count):
    size = lax.axis_size(axis)
    return lax.ppermute(x, axis, [(i, (i + count) % size) for i in range(size)])


def swap(x):
    return lax.ppermute(x, "pool", [(0, 1), (1, 0)])


def exchange(x, axis):
    return lax.all_to_all(x, axis, split_axis=0, concat_axis=0, tiled=True)


def attention_kernel(q_ref, kv_ref, o_ref):
    heads = q_ref.shape[1] // HD
    lane = lax.broadcasted_iota(jnp.int32, (q_ref.shape[0], HD), 1)
    stats = jnp.zeros(lane.shape, F32)
    for h in range(heads):
        cols = slice(h * HD, (h + 1) * HD)
        values = kv_ref[:, (heads + h) * HD : (heads + h + 1) * HD]
        scores = lax.dot_general(
            q_ref[:, cols], kv_ref[:, cols], (((1,), (1,)), ((), ())), preferred_element_type=F32
        ) * (1.0 / math.sqrt(HD))
        top = jnp.max(scores, axis=1, keepdims=True)
        weights = jnp.exp(scores - top)
        total = jnp.sum(weights, axis=1, keepdims=True)
        part = jnp.dot(weights.astype(BF16), values, preferred_element_type=F32)
        o_ref[:, cols] = (part / total).astype(BF16)
        rest = top + jnp.log(total)
        for k in range(3):
            term = rest.astype(BF16).astype(F32)
            stats = jnp.where(lane == 3 * h + k, term, stats)
            rest = rest - term
    o_ref[:, heads * HD :] = stats.astype(BF16)


def attend(queries, key_value):
    rows, depth = queries.shape
    return pl.pallas_call(
        attention_kernel,
        out_shape=jax.ShapeDtypeStruct((rows, depth + HD), BF16),
        compiler_params=pltpu.CompilerParams(vmem_limit_bytes=16 << 20),
        cost_estimate=pl.CostEstimate(
            flops=4 * rows * depth * key_value.shape[0],
            bytes_accessed=2 * key_value.size,
            transcendentals=0,
        ),
    )(queries, key_value)


def pack_weights(w_gate, w_up, w_down):
    pad = -w_down.shape[0] % 16
    return jnp.concatenate(
        [jnp.pad(w, ((0, pad), (0, 0))) for w in (w_gate.T, w_up.T, w_down)], 0
    )


def hidden_units(ids_ref, x, weights, route):
    hidden = weights[0].shape[0] // 2
    both = lax.dot_general(
        jnp.concatenate(weights, 0), x, (((1,), (1,)), ((), ())), preferred_element_type=F32
    )
    acts = []
    for i in range(len(weights)):
        scale = jnp.zeros((1, x.shape[0]), F32)
        for k in range(2):
            value = route[2 + k : 3 + k] + route[4 + k : 5 + k]
            scale += jnp.where(route[k : k + 1] == ids_ref[i].astype(F32), value, 0.0)
        gate = both[2 * i * hidden : (2 * i + 1) * hidden]
        up = both[(2 * i + 1) * hidden : (2 * i + 2) * hidden]
        acts.append((gate / (1.0 + jnp.exp(-gate)) * up * scale).astype(BF16))
    return jnp.concatenate(acts, 0)


def early_kernel(ids_ref, x_hbm, *refs):
    o_ref, x_ref, w_ref, sems = refs[-4:]
    parts = refs[:-4]
    width = w_ref.shape[2]
    copies = [pltpu.make_async_copy(x_hbm, x_ref, sems.at[len(parts)])]
    for i, part in enumerate(parts):
        copies.append(
            pltpu.make_async_copy(part.at[pl.ds(0, w_ref.shape[1])], w_ref.at[i], sems.at[i])
        )
    for copy in copies:
        copy.start()
    for copy in copies:
        copy.wait()
    o_ref[...] = hidden_units(
        ids_ref,
        x_ref[:, :width],
        [w_ref[i] for i in range(len(parts))],
        x_ref[:, width:].astype(F32).T,
    )


def late_kernel(count, ids_ref, x_hbm, units_ref, *refs):
    o_ref, x_ref, w_ref, act_ref, down_ref, sems = refs[-6:]
    parts = refs[:-6]
    width = w_ref.shape[2]
    hidden = w_ref.shape[1] // 2
    early = len(parts) - count
    x_copy = pltpu.make_async_copy(x_hbm, x_ref, sems.at[0])
    x_copy.start()
    wide = []
    for i, part in enumerate(parts[early:]):
        wide.append(
            pltpu.make_async_copy(part.at[pl.ds(0, 2 * hidden)], w_ref.at[i], sems.at[1 + i])
        )
        wide[i].start()
    tall = []
    for i, part in enumerate(parts):
        tall.append(
            pltpu.make_async_copy(
                part.at[pl.ds(2 * hidden, hidden)],
                down_ref.at[pl.ds(i * hidden, hidden)],
                sems.at[1 + count + i],
            )
        )
        tall[i].start()
    act_ref[: early * hidden] = units_ref[...]
    x_copy.wait()
    x = x_ref[:, :width]
    route = x_ref[:, width:].astype(F32).T
    each = 3
    for first in range(0, count, each):
        last = min(first + each, count)
        for i in range(first, last):
            wide[i].wait()
        act_ref[(early + first) * hidden : (early + last) * hidden] = hidden_units(
            ids_ref.at[pl.ds(first, last - first)],
            x,
            [w_ref[i] for i in range(first, last)],
            route,
        )
    for copy in tall:
        copy.wait()
    o_ref[...] = lax.dot_general(
        act_ref[...], down_ref[...], (((0,), (0,)), ((), ())), preferred_element_type=F32
    ).astype(BF16)


def ffn(ids, x, first, last):
    rows = x.shape[0]
    depth, width = first[0].shape
    hidden = depth // 3
    early, late = len(first), len(last)
    smem = pl.BlockSpec(memory_space=pltpu.SMEM)
    vmem = pl.BlockSpec(memory_space=pltpu.VMEM)
    whole = pl.BlockSpec(memory_space=pl.ANY)
    units = pl.pallas_call(
        early_kernel,
        out_shape=jax.ShapeDtypeStruct((early * hidden, rows), BF16),
        in_specs=[smem] + [whole] * (1 + early),
        out_specs=vmem,
        scratch_shapes=[
            pltpu.VMEM(x.shape, BF16),
            pltpu.VMEM((early, 2 * hidden, width), BF16),
            pltpu.SemaphoreType.DMA((early + 1,)),
        ],
        compiler_params=pltpu.CompilerParams(vmem_limit_bytes=30 << 20),
        cost_estimate=pl.CostEstimate(
            flops=16 * rows * width * depth * early,
            bytes_accessed=16 * width * depth * early,
            transcendentals=0,
        ),
    )(ids[:early], x, *first)
    return pl.pallas_call(
        functools.partial(late_kernel, late),
        out_shape=jax.ShapeDtypeStruct((rows, width), BF16),
        in_specs=[smem, whole, vmem] + [whole] * (early + late),
        out_specs=vmem,
        scratch_shapes=[
            pltpu.VMEM(x.shape, BF16),
            pltpu.VMEM((late, 2 * hidden, width), BF16),
            pltpu.VMEM(((early + late) * hidden, rows), BF16),
            pltpu.VMEM(((early + late) * hidden, width), BF16),
            pltpu.SemaphoreType.DMA((1 + early + 2 * late,)),
        ],
        compiler_params=pltpu.CompilerParams(vmem_limit_bytes=30 << 20),
        cost_estimate=pl.CostEstimate(
            flops=4 * rows * width * depth * late,
            bytes_accessed=2 * width * depth * (early + late),
            transcendentals=0,
        ),
    )(ids[early:], x, units, *first, *last)


def body(
    tokens,
    query_proj,
    key_proj,
    value_proj,
    w_out,
    modulation,
    expert_ids,
    gate_values,
    w_gate,
    w_up,
    w_down,
):
    rows, width = tokens.shape
    heads = query_proj.shape[1] // HD
    own_rows = rows // (2 * TP)
    pool = lax.axis_index("pool")
    tp = lax.axis_index("tp")
    group = pool * TP + tp

    packed = pack_weights(w_gate[0], w_up[0], w_down[0])
    before = shift(packed, "tp", 1)
    after = shift(packed, "tp", -1)

    queries = spread(query_proj, "y", Y).reshape(Y * rows, heads * HD)
    key_value = lax.all_gather(
        jnp.concatenate([key_proj, value_proj], 1), "z", axis=0, tiled=True
    )
    partial = attend(queries, key_value)

    before, after, partial = lax.optimization_barrier((before, after, partial))
    across = shift(before, "tp", 1)
    partial = exchange(partial.reshape(Y, rows, (heads + 1) * HD), "y").astype(F32)
    outs = []
    for h in range(heads):
        log_sum = partial[:, :, heads * HD + 3 * h : heads * HD + 3 * h + 3]
        log_sum = jnp.sum(log_sum, axis=2, keepdims=True)
        scale = jnp.exp(log_sum - jnp.max(log_sum, axis=0, keepdims=True))
        acc = jnp.sum(scale * partial[:, :, h * HD : (h + 1) * HD], axis=0)
        outs.append(acc / jnp.sum(scale, axis=0))
    heads_out = jnp.concatenate(outs, 1).astype(BF16)

    projected = jnp.dot(heads_out, w_out, preferred_element_type=F32).astype(BF16)
    projected = projected.reshape(2 * TP, own_rows, width)
    projected = exchange(projected, GROUP)
    attention = jnp.sum(projected.astype(F32), axis=0)
    own_tokens = lax.dynamic_slice_in_dim(tokens, group * own_rows, own_rows, 0).astype(F32)
    resid = own_tokens + modulation[0] * attention
    row_mean = jnp.mean(resid, axis=1, keepdims=True)
    row_square = jnp.mean(resid * resid, axis=1, keepdims=True)
    inv_dev = lax.rsqrt(row_square - row_mean * row_mean + 1e-06)
    normed = ((resid - row_mean) * inv_dev * (1.0 + modulation[2]) + modulation[1]).astype(BF16)

    own_ids = lax.dynamic_slice_in_dim(expert_ids, group * own_rows, own_rows, 0)
    own_gates = lax.dynamic_slice_in_dim(gate_values, group * own_rows, own_rows, 0)
    gates_hi = lax.reduce_precision(own_gates, 8, 7)
    gates_lo = own_gates - gates_hi
    route = jnp.concatenate(
        [own_ids.astype(BF16), gates_hi.astype(BF16), gates_lo.astype(BF16)], 1
    )
    route = jnp.pad(route, ((0, 0), (0, HD - route.shape[1])))
    sent = jnp.concatenate([normed, route], 1)
    copies = copies_of(sent, Z)
    copies = copies_of(exchange(copies, "z").reshape(Z * own_rows, width + HD), Y)
    packed, before, after, copies = lax.optimization_barrier((packed, before, after, copies))
    early = [packed, before, after]
    across_tied, _ = lax.optimization_barrier((across, copies))
    late = [across] + [swap(w) for w in early + [across_tied]]
    rows_in = exchange(copies, "y").reshape(Y * Z * own_rows, width + HD)
    near = (tp + jnp.array([0, TP - 1, 1, 2], jnp.int32)) % TP
    ids = jnp.concatenate([pool * TP + near, (1 - pool) * TP + near]).astype(jnp.int32)
    mixed = ffn(ids, rows_in, early, late)

    mixed = exchange(mixed.reshape(Y, Z * own_rows, width), "y")
    mixed = jnp.sum(mixed.astype(F32), axis=0).astype(BF16)
    mixed = exchange(mixed.reshape(Z, own_rows, width), "z")
    mixture = jnp.sum(mixed.astype(F32), axis=0)
    block_out = (resid + modulation[3] * mixture).astype(BF16)
    block_out = block_out.reshape(own_rows, 2 * TP, width // (2 * TP)).transpose(1, 0, 2)
    return exchange(block_out, GROUP).reshape(rows, width // (2 * TP))


def solution(mesh):
    split = Mesh(
        mesh.devices.reshape(2, Y, Z, TP), ("pool", "y", "z", "tp")
    )
    seq = ("y", "z")
    in_specs = (
        P(seq, None),
        P(seq, GROUP),
        P(seq, GROUP),
        P(seq, GROUP),
        P(GROUP, None),
        P(),
        P(seq, None),
        P(seq, None),
        P(GROUP, None, seq),
        P(GROUP, None, seq),
        P(GROUP, seq, None),
    )
    return jax.shard_map(
        body, mesh=split, in_specs=in_specs, out_specs=P(seq, GROUP), check_vma=False
    )
```

```python
import functools
import math

import jax
import jax.numpy as jnp
from jax import lax
from jax.experimental import pallas as pl
from jax.experimental.pallas import tpu as pltpu
from jax.sharding import Mesh
from jax.sharding import PartitionSpec as P

HD = 128
Y = 4
Z = 16
TP = 4
GROUP = ("pool", "tp")
F32 = jnp.float32
BF16 = jnp.bfloat16


def copies_of(x, count):
    return jnp.broadcast_to(x[None], (count,) + x.shape)


def spread(x, axis, count):
    return exchange(copies_of(x, count), axis)


def shift(x, axis, count):
    size = lax.axis_size(axis)
    return lax.ppermute(x, axis, [(i, (i + count) % size) for i in range(size)])


def swap(x):
    return lax.ppermute(x, "pool", [(0, 1), (1, 0)])


def exchange(x, axis):
    return lax.all_to_all(x, axis, split_axis=0, concat_axis=0, tiled=True)


def attention_kernel(q_ref, kv_ref, o_ref):
    heads = q_ref.shape[1] // HD
    lane = lax.broadcasted_iota(jnp.int32, (q_ref.shape[0], HD), 1)
    stats = jnp.zeros(lane.shape, F32)
    for h in range(heads):
        cols = slice(h * HD, (h + 1) * HD)
        values = kv_ref[:, (heads + h) * HD : (heads + h + 1) * HD]
        scores = lax.dot_general(
            q_ref[:, cols], kv_ref[:, cols], (((1,), (1,)), ((), ())), preferred_element_type=F32
        ) * (1.0 / math.sqrt(HD))
        top = jnp.max(scores, axis=1, keepdims=True)
        weights = jnp.exp(scores - top)
        total = jnp.sum(weights, axis=1, keepdims=True)
        part = jnp.dot(weights.astype(BF16), values, preferred_element_type=F32)
        o_ref[:, cols] = (part / total).astype(BF16)
        rest = top + jnp.log(total)
        for k in range(3):
            term = rest.astype(BF16).astype(F32)
            stats = jnp.where(lane == 3 * h + k, term, stats)
            rest = rest - term
    o_ref[:, heads * HD :] = stats.astype(BF16)


def attend(queries, key_value):
    rows, depth = queries.shape
    return pl.pallas_call(
        attention_kernel,
        out_shape=jax.ShapeDtypeStruct((rows, depth + HD), BF16),
        compiler_params=pltpu.CompilerParams(vmem_limit_bytes=16 << 20),
        cost_estimate=pl.CostEstimate(
            flops=4 * rows * depth * key_value.shape[0],
            bytes_accessed=2 * key_value.size,
            transcendentals=0,
        ),
    )(queries, key_value)


def pack_weights(w_gate, w_up, w_down):
    pad = -w_down.shape[0] % 16
    return jnp.concatenate(
        [jnp.pad(w, ((0, pad), (0, 0))) for w in (w_gate.T, w_up.T, w_down)], 0
    )


def hidden_units(ids_ref, x, weights, route):
    hidden = weights[0].shape[0] // 2
    both = lax.dot_general(
        jnp.concatenate(weights, 0), x, (((1,), (1,)), ((), ())), preferred_element_type=F32
    )
    acts = []
    for i in range(len(weights)):
        scale = jnp.zeros((1, x.shape[0]), F32)
        for k in range(2):
            value = route[2 + k : 3 + k] + route[4 + k : 5 + k]
            scale += jnp.where(route[k : k + 1] == ids_ref[i].astype(F32), value, 0.0)
        gate = both[2 * i * hidden : (2 * i + 1) * hidden]
        up = both[(2 * i + 1) * hidden : (2 * i + 2) * hidden]
        acts.append((gate / (1.0 + jnp.exp(-gate)) * up * scale).astype(BF16))
    return jnp.concatenate(acts, 0)


def early_kernel(ids_ref, x_ref, *refs):
    o_ref, w_ref, sems = refs[-3:]
    parts = refs[:-3]
    width = w_ref.shape[2]
    copies = []
    for i, part in enumerate(parts):
        copies.append(
            pltpu.make_async_copy(part.at[pl.ds(0, w_ref.shape[1])], w_ref.at[i], sems.at[i])
        )
    for copy in copies:
        copy.start()
    for copy in copies:
        copy.wait()
    o_ref[...] = hidden_units(
        ids_ref,
        x_ref[:, :width],
        [w_ref[i] for i in range(len(parts))],
        x_ref[:, width:].astype(F32).T,
    )


def late_kernel(count, ids_ref, x_ref, units_ref, *refs):
    o_ref, w_ref, act_ref, down_ref, sems = refs[-5:]
    parts = refs[:-5]
    width = w_ref.shape[2]
    hidden = w_ref.shape[1] // 2
    early = len(parts) - count
    wide = []
    for i, part in enumerate(parts[early:]):
        wide.append(
            pltpu.make_async_copy(part.at[pl.ds(0, 2 * hidden)], w_ref.at[i], sems.at[i])
        )
        wide[i].start()
    tall = []
    for i, part in enumerate(parts):
        tall.append(
            pltpu.make_async_copy(
                part.at[pl.ds(2 * hidden, hidden)],
                down_ref.at[pl.ds(i * hidden, hidden)],
                sems.at[count + i],
            )
        )
        tall[i].start()
    act_ref[: early * hidden] = units_ref[...]
    x = x_ref[:, :width]
    route = x_ref[:, width:].astype(F32).T
    each = 3
    for first in range(0, count, each):
        last = min(first + each, count)
        for i in range(first, last):
            wide[i].wait()
        act_ref[(early + first) * hidden : (early + last) * hidden] = hidden_units(
            ids_ref.at[pl.ds(first, last - first)],
            x,
            [w_ref[i] for i in range(first, last)],
            route,
        )
    for copy in tall:
        copy.wait()
    o_ref[...] = lax.dot_general(
        act_ref[...], down_ref[...], (((0,), (0,)), ((), ())), preferred_element_type=F32
    ).astype(BF16)


def ffn(ids, x, first, last):
    rows = x.shape[0]
    depth, width = first[0].shape
    hidden = depth // 3
    early, late = len(first), len(last)
    smem = pl.BlockSpec(memory_space=pltpu.SMEM)
    vmem = pl.BlockSpec(memory_space=pltpu.VMEM)
    whole = pl.BlockSpec(memory_space=pl.ANY)
    units = pl.pallas_call(
        early_kernel,
        out_shape=jax.ShapeDtypeStruct((early * hidden, rows), BF16),
        in_specs=[smem, vmem] + [whole] * early,
        out_specs=vmem,
        scratch_shapes=[
            pltpu.VMEM((early, 2 * hidden, width), BF16),
            pltpu.SemaphoreType.DMA((early,)),
        ],
        compiler_params=pltpu.CompilerParams(vmem_limit_bytes=30 << 20),
        cost_estimate=pl.CostEstimate(
            flops=16 * rows * width * depth * early,
            bytes_accessed=16 * width * depth * early,
            transcendentals=0,
        ),
    )(ids[:early], x, *first)
    return pl.pallas_call(
        functools.partial(late_kernel, late),
        out_shape=jax.ShapeDtypeStruct((rows, width), BF16),
        in_specs=[smem, vmem, vmem] + [whole] * (early + late),
        out_specs=vmem,
        scratch_shapes=[
            pltpu.VMEM((late, 2 * hidden, width), BF16),
            pltpu.VMEM(((early + late) * hidden, rows), BF16),
            pltpu.VMEM(((early + late) * hidden, width), BF16),
            pltpu.SemaphoreType.DMA((early + 2 * late,)),
        ],
        compiler_params=pltpu.CompilerParams(vmem_limit_bytes=30 << 20),
        cost_estimate=pl.CostEstimate(
            flops=4 * rows * width * depth * late,
            bytes_accessed=2 * width * depth * (early + late),
            transcendentals=0,
        ),
    )(ids[early:], x, units, *first, *last)


def body(
    tokens,
    query_proj,
    key_proj,
    value_proj,
    w_out,
    modulation,
    expert_ids,
    gate_values,
    w_gate,
    w_up,
    w_down,
):
    rows, width = tokens.shape
    heads = query_proj.shape[1] // HD
    own_rows = rows // (2 * TP)
    pool = lax.axis_index("pool")
    tp = lax.axis_index("tp")
    group = pool * TP + tp

    packed = pack_weights(w_gate[0], w_up[0], w_down[0])
    before = shift(packed, "tp", 1)
    after = shift(packed, "tp", -1)

    queries = spread(query_proj, "y", Y).reshape(Y * rows, heads * HD)
    key_value = lax.all_gather(
        jnp.concatenate([key_proj, value_proj], 1), "z", axis=0, tiled=True
    )
    partial = attend(queries, key_value)

    before, after, partial = lax.optimization_barrier((before, after, partial))
    across = shift(before, "tp", 1)
    partial = exchange(partial.reshape(Y, rows, (heads + 1) * HD), "y").astype(F32)
    outs = []
    for h in range(heads):
        log_sum = partial[:, :, heads * HD + 3 * h : heads * HD + 3 * h + 3]
        log_sum = jnp.sum(log_sum, axis=2, keepdims=True)
        scale = jnp.exp(log_sum - jnp.max(log_sum, axis=0, keepdims=True))
        acc = jnp.sum(scale * partial[:, :, h * HD : (h + 1) * HD], axis=0)
        outs.append(acc / jnp.sum(scale, axis=0))
    heads_out = jnp.concatenate(outs, 1).astype(BF16)

    projected = jnp.dot(heads_out, w_out, preferred_element_type=F32).astype(BF16)
    projected = projected.reshape(2 * TP, own_rows, width)
    projected = exchange(projected, GROUP)
    attention = jnp.sum(projected.astype(F32), axis=0)
    own_tokens = lax.dynamic_slice_in_dim(tokens, group * own_rows, own_rows, 0).astype(F32)
    resid = own_tokens + modulation[0] * attention
    row_mean = jnp.mean(resid, axis=1, keepdims=True)
    row_square = jnp.mean(resid * resid, axis=1, keepdims=True)
    inv_dev = lax.rsqrt(row_square - row_mean * row_mean + 1e-06)
    normed = ((resid - row_mean) * inv_dev * (1.0 + modulation[2]) + modulation[1]).astype(BF16)

    own_ids = lax.dynamic_slice_in_dim(expert_ids, group * own_rows, own_rows, 0)
    own_gates = lax.dynamic_slice_in_dim(gate_values, group * own_rows, own_rows, 0)
    gates_hi = lax.reduce_precision(own_gates, 8, 7)
    gates_lo = own_gates - gates_hi
    route = jnp.concatenate(
        [own_ids.astype(BF16), gates_hi.astype(BF16), gates_lo.astype(BF16)], 1
    )
    route = jnp.pad(route, ((0, 0), (0, HD - route.shape[1])))
    sent = jnp.concatenate([normed, route], 1)
    copies = copies_of(sent, Z)
    copies = copies_of(exchange(copies, "z").reshape(Z * own_rows, width + HD), Y)
    packed, before, after, copies = lax.optimization_barrier((packed, before, after, copies))
    early = [packed, before, after]
    across_tied, _ = lax.optimization_barrier((across, copies))
    late = [across] + [swap(w) for w in early + [across_tied]]
    rows_in = exchange(copies, "y").reshape(Y * Z * own_rows, width + HD)
    near = (tp + jnp.array([0, TP - 1, 1, 2], jnp.int32)) % TP
    ids = jnp.concatenate([pool * TP + near, (1 - pool) * TP + near]).astype(jnp.int32)
    mixed = ffn(ids, rows_in, early, late)

    mixed = exchange(mixed.reshape(Y, Z * own_rows, width), "y")
    mixed = jnp.sum(mixed.astype(F32), axis=0).astype(BF16)
    mixed = exchange(mixed.reshape(Z, own_rows, width), "z")
    mixture = jnp.sum(mixed.astype(F32), axis=0)
    block_out = (resid + modulation[3] * mixture).astype(BF16)
    block_out = block_out.reshape(own_rows, 2 * TP, width // (2 * TP)).transpose(1, 0, 2)
    return exchange(block_out, GROUP).reshape(rows, width // (2 * TP))


def solution(mesh):
    split = Mesh(
        mesh.devices.reshape(2, Y, Z, TP), ("pool", "y", "z", "tp")
    )
    seq = ("y", "z")
    in_specs = (
        P(seq, None),
        P(seq, GROUP),
        P(seq, GROUP),
        P(seq, GROUP),
        P(GROUP, None),
        P(),
        P(seq, None),
        P(seq, None),
        P(GROUP, None, seq),
        P(GROUP, None, seq),
        P(GROUP, seq, None),
    )
    return jax.shard_map(
        body, mesh=split, in_specs=in_specs, out_specs=P(seq, GROUP), check_vma=False
    )
```

```python
import functools
import math

import jax
import jax.numpy as jnp
from jax import lax
from jax.experimental import pallas as pl
from jax.experimental.pallas import tpu as pltpu
from jax.sharding import Mesh
from jax.sharding import PartitionSpec as P

HD = 128
Y = 4
Z = 16
TP = 4
GROUP = ("pool", "tp")
F32 = jnp.float32
BF16 = jnp.bfloat16


def copies_of(x, count):
    return jnp.broadcast_to(x[None], (count,) + x.shape)


def spread(x, axis, count):
    return exchange(copies_of(x, count), axis)


def shift(x, axis, count):
    size = lax.axis_size(axis)
    return lax.ppermute(x, axis, [(i, (i + count) % size) for i in range(size)])


def swap(x):
    return lax.ppermute(x, "pool", [(0, 1), (1, 0)])


def exchange(x, axis):
    return lax.all_to_all(x, axis, split_axis=0, concat_axis=0, tiled=True)


def attention_kernel(q_ref, kv_ref, o_ref):
    heads = q_ref.shape[1] // HD
    lane = lax.broadcasted_iota(jnp.int32, (q_ref.shape[0], HD), 1)
    stats = jnp.zeros(lane.shape, F32)
    for h in range(heads):
        cols = slice(h * HD, (h + 1) * HD)
        values = kv_ref[:, (heads + h) * HD : (heads + h + 1) * HD]
        scores = lax.dot_general(
            q_ref[:, cols], kv_ref[:, cols], (((1,), (1,)), ((), ())), preferred_element_type=F32
        ) * (1.0 / math.sqrt(HD))
        top = jnp.max(scores, axis=1, keepdims=True)
        weights = jnp.exp(scores - top)
        total = jnp.sum(weights, axis=1, keepdims=True)
        part = jnp.dot(weights.astype(BF16), values, preferred_element_type=F32)
        o_ref[:, cols] = (part / total).astype(BF16)
        rest = top + jnp.log(total)
        for k in range(3):
            term = rest.astype(BF16).astype(F32)
            stats = jnp.where(lane == 3 * h + k, term, stats)
            rest = rest - term
    o_ref[:, heads * HD :] = stats.astype(BF16)


def attend(queries, key_value):
    rows, depth = queries.shape
    return pl.pallas_call(
        attention_kernel,
        out_shape=jax.ShapeDtypeStruct((rows, depth + HD), BF16),
        compiler_params=pltpu.CompilerParams(vmem_limit_bytes=16 << 20),
        cost_estimate=pl.CostEstimate(
            flops=4 * rows * depth * key_value.shape[0],
            bytes_accessed=2 * key_value.size,
            transcendentals=0,
        ),
    )(queries, key_value)


def pack_weights(w_gate, w_up, w_down):
    pad = -w_down.shape[0] % 16
    return jnp.concatenate(
        [jnp.pad(w, ((0, pad), (0, 0))) for w in (w_gate.T, w_up.T, w_down)], 0
    )


def hidden_units(ids_ref, x, weights, route):
    hidden = weights[0].shape[0] // 2
    both = lax.dot_general(
        jnp.concatenate(weights, 0), x, (((1,), (1,)), ((), ())), preferred_element_type=F32
    )
    acts = []
    for i in range(len(weights)):
        scale = jnp.zeros((1, x.shape[0]), F32)
        for k in range(2):
            value = route[2 + k : 3 + k] + route[4 + k : 5 + k]
            scale += jnp.where(route[k : k + 1] == ids_ref[i].astype(F32), value, 0.0)
        gate = both[2 * i * hidden : (2 * i + 1) * hidden]
        up = both[(2 * i + 1) * hidden : (2 * i + 2) * hidden]
        acts.append((gate / (1.0 + jnp.exp(-gate)) * up * scale).astype(BF16))
    return jnp.concatenate(acts, 0)


def early_kernel(ids_ref, x_ref, *refs):
    o_ref, w_ref, sems = refs[-3:]
    parts = refs[:-3]
    width = w_ref.shape[2]
    copies = []
    for i, part in enumerate(parts):
        copies.append(
            pltpu.make_async_copy(part.at[pl.ds(0, w_ref.shape[1])], w_ref.at[i], sems.at[i])
        )
    for copy in copies:
        copy.start()
    for copy in copies:
        copy.wait()
    o_ref[...] = hidden_units(
        ids_ref,
        x_ref[:, :width],
        [w_ref[i] for i in range(len(parts))],
        x_ref[:, width:].astype(F32).T,
    )


def late_kernel(count, ids_ref, x_ref, units_ref, *refs):
    o_ref, w_ref, act_ref, down_ref, sems = refs[-5:]
    parts = refs[:-5]
    width = w_ref.shape[2]
    hidden = w_ref.shape[1] // 2
    early = len(parts) - count
    wide = []
    for i, part in enumerate(parts[early:]):
        wide.append(
            pltpu.make_async_copy(part.at[pl.ds(0, 2 * hidden)], w_ref.at[i], sems.at[i])
        )
        wide[i].start()
    tall = []
    for i, part in enumerate(parts):
        tall.append(
            pltpu.make_async_copy(
                part.at[pl.ds(2 * hidden, hidden)],
                down_ref.at[pl.ds(i * hidden, hidden)],
                sems.at[count + i],
            )
        )
        tall[i].start()
    act_ref[: early * hidden] = units_ref[...]
    x = x_ref[:, :width]
    route = x_ref[:, width:].astype(F32).T
    each = 5
    for first in range(0, count, each):
        last = min(first + each, count)
        for i in range(first, last):
            wide[i].wait()
        act_ref[(early + first) * hidden : (early + last) * hidden] = hidden_units(
            ids_ref.at[pl.ds(first, last - first)],
            x,
            [w_ref[i] for i in range(first, last)],
            route,
        )
    for copy in tall:
        copy.wait()
    o_ref[...] = lax.dot_general(
        act_ref[...], down_ref[...], (((0,), (0,)), ((), ())), preferred_element_type=F32
    ).astype(BF16)


def ffn(ids, x, first, last):
    rows = x.shape[0]
    depth, width = first[0].shape
    hidden = depth // 3
    early, late = len(first), len(last)
    smem = pl.BlockSpec(memory_space=pltpu.SMEM)
    vmem = pl.BlockSpec(memory_space=pltpu.VMEM)
    whole = pl.BlockSpec(memory_space=pl.ANY)
    units = pl.pallas_call(
        early_kernel,
        out_shape=jax.ShapeDtypeStruct((early * hidden, rows), BF16),
        in_specs=[smem, vmem] + [whole] * early,
        out_specs=vmem,
        scratch_shapes=[
            pltpu.VMEM((early, 2 * hidden, width), BF16),
            pltpu.SemaphoreType.DMA((early,)),
        ],
        compiler_params=pltpu.CompilerParams(vmem_limit_bytes=30 << 20),
        cost_estimate=pl.CostEstimate(
            flops=16 * rows * width * depth * early,
            bytes_accessed=16 * width * depth * early,
            transcendentals=0,
        ),
    )(ids[:early], x, *first)
    return pl.pallas_call(
        functools.partial(late_kernel, late),
        out_shape=jax.ShapeDtypeStruct((rows, width), BF16),
        in_specs=[smem, vmem, vmem] + [whole] * (early + late),
        out_specs=vmem,
        scratch_shapes=[
            pltpu.VMEM((late, 2 * hidden, width), BF16),
            pltpu.VMEM(((early + late) * hidden, rows), BF16),
            pltpu.VMEM(((early + late) * hidden, width), BF16),
            pltpu.SemaphoreType.DMA((early + 2 * late,)),
        ],
        compiler_params=pltpu.CompilerParams(vmem_limit_bytes=30 << 20),
        cost_estimate=pl.CostEstimate(
            flops=4 * rows * width * depth * late,
            bytes_accessed=2 * width * depth * (early + late),
            transcendentals=0,
        ),
    )(ids[early:], x, units, *first, *last)


def body(
    tokens,
    query_proj,
    key_proj,
    value_proj,
    w_out,
    modulation,
    expert_ids,
    gate_values,
    w_gate,
    w_up,
    w_down,
):
    rows, width = tokens.shape
    heads = query_proj.shape[1] // HD
    own_rows = rows // (2 * TP)
    pool = lax.axis_index("pool")
    tp = lax.axis_index("tp")
    group = pool * TP + tp

    packed = pack_weights(w_gate[0], w_up[0], w_down[0])
    before = shift(packed, "tp", 1)
    after = shift(packed, "tp", -1)

    queries = spread(query_proj, "y", Y).reshape(Y * rows, heads * HD)
    key_value = lax.all_gather(
        jnp.concatenate([key_proj, value_proj], 1), "z", axis=0, tiled=True
    )
    partial = attend(queries, key_value)

    before, after, partial = lax.optimization_barrier((before, after, partial))
    across = shift(before, "tp", 1)
    partial = exchange(partial.reshape(Y, rows, (heads + 1) * HD), "y").astype(F32)
    outs = []
    for h in range(heads):
        log_sum = partial[:, :, heads * HD + 3 * h : heads * HD + 3 * h + 3]
        log_sum = jnp.sum(log_sum, axis=2, keepdims=True)
        scale = jnp.exp(log_sum - jnp.max(log_sum, axis=0, keepdims=True))
        acc = jnp.sum(scale * partial[:, :, h * HD : (h + 1) * HD], axis=0)
        outs.append(acc / jnp.sum(scale, axis=0))
    heads_out = jnp.concatenate(outs, 1).astype(BF16)

    projected = jnp.dot(heads_out, w_out, preferred_element_type=F32).astype(BF16)
    projected = projected.reshape(2 * TP, own_rows, width)
    projected = exchange(projected, GROUP)
    attention = jnp.sum(projected.astype(F32), axis=0)
    own_tokens = lax.dynamic_slice_in_dim(tokens, group * own_rows, own_rows, 0).astype(F32)
    resid = own_tokens + modulation[0] * attention
    row_mean = jnp.mean(resid, axis=1, keepdims=True)
    row_square = jnp.mean(resid * resid, axis=1, keepdims=True)
    inv_dev = lax.rsqrt(row_square - row_mean * row_mean + 1e-06)
    normed = ((resid - row_mean) * inv_dev * (1.0 + modulation[2]) + modulation[1]).astype(BF16)

    own_ids = lax.dynamic_slice_in_dim(expert_ids, group * own_rows, own_rows, 0)
    own_gates = lax.dynamic_slice_in_dim(gate_values, group * own_rows, own_rows, 0)
    gates_hi = lax.reduce_precision(own_gates, 8, 7)
    gates_lo = own_gates - gates_hi
    route = jnp.concatenate(
        [own_ids.astype(BF16), gates_hi.astype(BF16), gates_lo.astype(BF16)], 1
    )
    route = jnp.pad(route, ((0, 0), (0, HD - route.shape[1])))
    sent = jnp.concatenate([normed, route], 1)
    copies = copies_of(sent, Z)
    copies = copies_of(exchange(copies, "z").reshape(Z * own_rows, width + HD), Y)
    packed, before, after, copies = lax.optimization_barrier((packed, before, after, copies))
    early = [packed, before, after]
    across_tied, _ = lax.optimization_barrier((across, copies))
    late = [across] + [swap(w) for w in early + [across_tied]]
    rows_in = exchange(copies, "y").reshape(Y * Z * own_rows, width + HD)
    near = (tp + jnp.array([0, TP - 1, 1, 2], jnp.int32)) % TP
    ids = jnp.concatenate([pool * TP + near, (1 - pool) * TP + near]).astype(jnp.int32)
    mixed = ffn(ids, rows_in, early, late)

    mixed = exchange(mixed.reshape(Y, Z * own_rows, width), "y")
    mixed = jnp.sum(mixed.astype(F32), axis=0).astype(BF16)
    mixed = exchange(mixed.reshape(Z, own_rows, width), "z")
    mixture = jnp.sum(mixed.astype(F32), axis=0)
    block_out = (resid + modulation[3] * mixture).astype(BF16)
    block_out = block_out.reshape(own_rows, 2 * TP, width // (2 * TP)).transpose(1, 0, 2)
    return exchange(block_out, GROUP).reshape(rows, width // (2 * TP))


def solution(mesh):
    split = Mesh(
        mesh.devices.reshape(2, Y, Z, TP), ("pool", "y", "z", "tp")
    )
    seq = ("y", "z")
    in_specs = (
        P(seq, None),
        P(seq, GROUP),
        P(seq, GROUP),
        P(seq, GROUP),
        P(GROUP, None),
        P(),
        P(seq, None),
        P(seq, None),
        P(GROUP, None, seq),
        P(GROUP, None, seq),
        P(GROUP, seq, None),
    )
    return jax.shard_map(
        body, mesh=split, in_specs=in_specs, out_specs=P(seq, GROUP), check_vma=False
    )
```
